32 devices in a mesh: dp: 4 (over x, core), fsdp: 8 (over z, y).
Axes of the slice: x: 2, y: 2, z: 4, core: 2. Of those that a mesh axis runs over, the one named last changes fastest.
Arguments:
- tokens: bfloat16 [32, 256, 1024], P(('dp', 'fsdp')), may hold values from -6 to 6
- memory: bfloat16 [32, 256, 1024], P(('dp', 'fsdp')), may hold values from -6 to 6
- token_segments: int32 [32, 256], P(('dp', 'fsdp')), may hold values from 0 to 3, never falling along the last dimension, each value on 1 to 128 neighbouring positions
- memory_segments: int32 [32, 256], P(('dp', 'fsdp')), may hold values from 0 to 3, never falling along the last dimension, each value on 1 to 128 neighbouring positions
- padding: int32 [32, 256], P(('dp', 'fsdp')), may hold values 0 or 1
- self_project: bfloat16 [3, 1024, 1024], P(None, ('dp', 'fsdp')), may hold values from -0.1875 to 0.1875
- self_output: bfloat16 [1024, 1024], P(('dp', 'fsdp')), may hold values from -0.75 to 0.75
- cross_project: bfloat16 [3, 1024, 1024], P(None, ('dp', 'fsdp')), may hold values from -0.1875 to 0.1875
- cross_output: bfloat16 [1024, 1024], P(('dp', 'fsdp')), may hold values from -0.75 to 0.75
- widen_weight: bfloat16 [1024, 4096], P(('dp', 'fsdp')), may hold values from -0.1875 to 0.1875
- narrow_weight: bfloat16 [4096, 1024], P(('dp', 'fsdp')), may hold values from -0.1875 to 0.1875
- norm_gain: bfloat16 [3, 1024], P(None, ('dp', 'fsdp')), may hold values from 0.5 to 1.5
- norm_bias: bfloat16 [3, 1024], P(None, ('dp', 'fsdp')), may hold values from -2 to 2
- grad_out: bfloat16 [32, 256, 1024], P(('dp', 'fsdp')), may hold values from -6 to 6
Outputs:
- layer_out: bfloat16 [32, 256, 1024], P(('dp', 'fsdp'))
- grad_tokens: float32 [32, 256, 1024], P(('dp', 'fsdp'))
- grad_memory: float32 [32, 256, 1024], P(('dp', 'fsdp'))
- grad_self_project: float32 [3, 1024, 1024], P(None, ('dp', 'fsdp'))
- grad_self_output: float32 [1024, 1024], P(('dp', 'fsdp'))
- grad_cross_project: float32 [3, 1024, 1024], P(None, ('dp', 'fsdp'))
- grad_cross_output: float32 [1024, 1024], P(('dp', 'fsdp'))
- grad_widen: float32 [1024, 4096], P(('dp', 'fsdp'))
- grad_narrow: float32 [4096, 1024], P(('dp', 'fsdp'))
- grad_norm_gain: float32 [3, 1024], P(None, ('dp', 'fsdp'))
- grad_norm_bias: float32 [3, 1024], P(None, ('dp', 'fsdp'))
The draws below stay inside these ranges and needn't reach their ends.
Inputs may be any that keep to these rules, and one draw needn't show every extreme that they name: `token_segments`: each row holds all 4 segments in order, one of them 256 // 2 tokens long. `memory_segments`: each row holds all 4 segments in order, one of them 256 // 2 tokens long.
All inputs are finite; a program needn't handle non-finite values. No bound on the sum of `padding` on one device may be relied on, other than what follows from the above.
Results may differ from the reference program's by a relative error of at most 0.013.
Values may be sent and summed in bfloat16 or wider, within the bound.
No kernel may reach another device: no remote copies, remote signals or barrier semaphores. Data moves between devices by JAX's collectives and lax.ppermute only.
A program may use at most 256 MiB of HBM per device.

```python
import math
import jax
import jax.numpy as jnp
import numpy as np
from jax import lax

HEADS = 16
HEAD = 64
D = 1024
FF = 4096
SEQ = 256
SEGS = 4
ROWS = 32


def place_ends(drawn, rng, least, high):
    longest = drawn.shape.index(max(drawn.shape))
    spots = []
    for shift in (0, 1):
        where = [jax.random.randint(jax.random.fold_in(rng, axis), (), 0, length) for axis, length in enumerate(drawn.shape)]
        where[longest] = (where[longest] + shift) % drawn.shape[longest]
        spots.append(tuple(where))
    return drawn.at[spots[0]].set(least).at[spots[1]].set(high)


def shard_levels(own_key, shape, cuts, smallest, high):
    factor_of, own = 1.0, jax.random.fold_in(own_key, 6)
    for position, parts in cuts:
        draws = jnp.exp(jax.random.uniform(jax.random.fold_in(own, position), (parts,), jnp.float32, smallest / len(cuts), high / len(cuts)))
        factor_of = factor_of * jnp.repeat(draws, shape[position] // parts).reshape([-1 if axis == position else 1 for axis in range(len(shape))])
    return factor_of


def profile(number_of, total, most, slope):
    weights = [(1 << 20) // math.isqrt(standing ** slope) + 1 for standing in range(2, number_of + 1)]
    spare, counts = total - most - (number_of - 1), [1] * (number_of - 1)
    while spare > 0:
        free = [i for i in range(number_of - 1) if counts[i] < most]
        whole, budget = sum([weights[i] for i in free]), spare
        for i in free:
            addition = min(most - counts[i], max(1, budget * weights[i] // whole), spare)
            counts[i] = counts[i] + addition
            spare = spare - addition
    return np.array([most] + counts)


def uneven_parts(own_key, number_of, total, reach, skew):
    if number_of == 2:
        one = jax.random.randint(own_key, (), max(1, total - reach), min(reach, total - 1) + 1)
        return jnp.stack([one, total - one])
    tallies = jnp.asarray(profile(number_of, total, reach, skew), jnp.int32)
    couples = (number_of - 1) // 2
    source_of, receiver = tallies[1:1 + 2 * couples:2], tallies[2:2 + 2 * couples:2]
    slack = jnp.minimum(source_of - 1, reach - receiver)
    passed = jax.random.randint(jax.random.fold_in(own_key, 1), (couples,), 0, 1 << 20) % (slack + 1)
    tallies = tallies.at[1:1 + 2 * couples:2].set(source_of - passed).at[2:2 + 2 * couples:2].set(receiver + passed)
    return tallies[jax.random.permutation(jax.random.fold_in(own_key, 2), number_of)]


def normal_values(own_key, dims, deviation, reach, cuts=(), held_as=jnp.bfloat16):
    result = deviation * jax.random.normal(own_key, dims, jnp.float32)
    if cuts:
        result = result * shard_levels(own_key, dims, cuts, -0.22, 0.18)
    return jnp.clip(result, -reach, reach).astype(held_as)


def setup_inputs(seed: int = 0) -> dict:
    arg_keys = jax.random.split(jax.random.key(seed), 15)
    return {
        "tokens": normal_values(arg_keys[0], (ROWS, SEQ, D), 1.0, 6.0, ((0, 32),)),
        "memory": normal_values(arg_keys[1], (ROWS, SEQ, D), 1.0, 6.0, ((0, 32),)),
        "token_segments": jax.vmap(lambda own: jnp.searchsorted(jnp.cumsum(uneven_parts(own, SEGS, SEQ, SEQ // 2, 0)), jnp.arange(SEQ), side="right"))(jax.random.split(arg_keys[2], ROWS)).reshape((ROWS, SEQ)).astype(jnp.int32),
        "memory_segments": jax.vmap(lambda own: jnp.searchsorted(jnp.cumsum(uneven_parts(own, SEGS, SEQ, SEQ // 2, 0)), jnp.arange(SEQ), side="right"))(jax.random.split(arg_keys[3], ROWS)).reshape((ROWS, SEQ)).astype(jnp.int32),
        "padding": place_ends((jax.random.randint(arg_keys[4], (ROWS, SEQ), 0, 8) < 7).astype(jnp.int32), jax.random.fold_in(arg_keys[4], 1), 0, 1),
        "self_project": normal_values(arg_keys[5], (3, D, D), D ** -0.5, 0.1875, ((1, 32),)),
        "self_output": normal_values(arg_keys[6], (D, D), (D // 16) ** -0.5, 0.75, ((0, 32),)),
        "cross_project": normal_values(arg_keys[7], (3, D, D), D ** -0.5, 0.1875, ((1, 32),)),
        "cross_output": normal_values(arg_keys[8], (D, D), (D // 16) ** -0.5, 0.75, ((0, 32),)),
        "widen_weight": normal_values(arg_keys[9], (D, FF), D ** -0.5, 0.1875, ((0, 32),)),
        "narrow_weight": normal_values(arg_keys[10], (FF, D), (FF // 4) ** -0.5, 0.1875, ((0, 32),)),
        "norm_gain": jnp.clip(1.0 + 0.1 * jax.random.normal(arg_keys[11], (3, D), jnp.float32), 0.5, 1.5).astype(jnp.bfloat16),
        "norm_bias": normal_values(arg_keys[12], (3, D), 0.3, 2.0, ((1, 32),)),
        "grad_out": normal_values(arg_keys[13], (ROWS, SEQ, D), 1.0, 6.0, ((0, 32),)),
    }


@jax.custom_vjp
def low(v):
    return lax.optimization_barrier(v.astype(jnp.bfloat16)).astype(jnp.float32)

@jax.custom_vjp
def low_back(v):
    return v

def low_keep(v):
    return (low(v), None)

def low_pass(kept, grad):
    return (grad,)

def back_keep(v):
    return (v, None)

def back_low(kept, grad):
    return (low(grad),)
low.defvjp(low_keep, low_pass)
low_back.defvjp(back_keep, back_low)
ALPHA = (3.0 * 200.0) ** 0.25
EPSILON = 1e-05
MASKED = -1e+30
HIGHEST = lax.Precision.HIGHEST

def both_ways(values_in):
    return low(low_back(values_in))

def product(first_side, other_side):
    return jnp.dot(first_side, other_side, precision=HIGHEST)

def normalize(values_in, scale_row, shift_row):
    average = lax.optimization_barrier(jnp.mean(values_in, axis=-1, keepdims=True))
    centred = values_in - average
    spread = lax.optimization_barrier(jnp.mean(centred * centred, axis=-1, keepdims=True))
    return centred * lax.rsqrt(spread + EPSILON) * scale_row + shift_row

def attend(queries, key_rows, values, allowed):
    length = queries.shape[0]
    key_count = key_rows.shape[0]
    head_query = queries.reshape(length, HEADS, HEAD)
    head_key = key_rows.reshape(key_count, HEADS, HEAD)
    head_value = values.reshape(key_count, HEADS, HEAD)
    scores = low_back(jnp.einsum('qhd,khd->hqk', head_query, head_key, precision=HIGHEST) * HEAD ** (-0.5))
    scores = jnp.where(allowed[None], scores, MASKED)
    largest = lax.optimization_barrier(jnp.max(scores, axis=-1, keepdims=True))
    exponentials = jnp.exp(scores - largest)
    weights = low(exponentials / lax.optimization_barrier(jnp.sum(exponentials, axis=-1, keepdims=True)))
    mixed = jnp.einsum('hqk,khd->qhd', weights, head_value, precision=HIGHEST)
    return both_ways(mixed.reshape(length, HEADS * HEAD))

def decoder_row(row_items, weight_values):
    row_in, memory_row, segment_row, memory_ids, pad_row = row_items
    self_stack, self_final, cross_stack, cross_final, widen_full, narrow_full, gain_values, bias_values = weight_values
    places = jnp.arange(segment_row.shape[0])
    diagonal = places[None, :] == places[:, None]
    live_keys = pad_row == 1
    self_allowed = (segment_row[:, None] == segment_row[None, :]) & (places[None, :] <= places[:, None]) & (live_keys[None, :] | diagonal)
    cross_allowed = segment_row[:, None] == memory_ids[None, :]
    inputs = low(row_in)
    self_mixed = attend(both_ways(product(inputs, self_stack[0])), both_ways(product(inputs, self_stack[1])), both_ways(product(inputs, self_stack[2])), self_allowed)
    pre_one = ALPHA * row_in + low_back(product(self_mixed, self_final))
    first_out = normalize(pre_one, gain_values[0], bias_values[0])
    first_low = low(first_out)
    cross_mixed = attend(both_ways(product(first_low, cross_stack[0])), both_ways(product(memory_row, cross_stack[1])), both_ways(product(memory_row, cross_stack[2])), cross_allowed)
    pre_two = ALPHA * first_out + low_back(product(cross_mixed, cross_final))
    second = normalize(pre_two, gain_values[1], bias_values[1])
    second_low = low(second)
    hidden = low_back(product(second_low, widen_full))
    active = low(jax.nn.gelu(hidden))
    pre_three = ALPHA * second + low_back(product(active, narrow_full))
    third_out = normalize(pre_three, gain_values[2], bias_values[2])
    return third_out * pad_row.astype(third_out.dtype)[:, None]

def reference(tokens, memory, token_segments, memory_segments, padding, self_project, self_output, cross_project, cross_output, widen_weight, narrow_weight, norm_gain, norm_bias, grad_out):
    weights = (self_project.astype(jnp.float32), self_output.astype(jnp.float32), cross_project.astype(jnp.float32), cross_output.astype(jnp.float32), widen_weight.astype(jnp.float32), narrow_weight.astype(jnp.float32), norm_gain.astype(jnp.float32), norm_bias.astype(jnp.float32))

    def forward(token_values, memory_values, weight_values):

        def one_row(row_items):
            return decoder_row(row_items, weight_values)
        return lax.map(jax.checkpoint(one_row), (token_values, memory_values, token_segments, memory_segments, padding))
    layer_values, pullback = jax.vjp(forward, tokens.astype(jnp.float32), memory.astype(jnp.float32), weights)
    grad_tokens, grad_memory, grad_weights = pullback(grad_out.astype(jnp.float32))
    return (layer_values.astype(jnp.bfloat16), grad_tokens, grad_memory, grad_weights[0], grad_weights[1], grad_weights[2], grad_weights[3], grad_weights[4], grad_weights[5], grad_weights[6], grad_weights[7])
```

```python
import functools

import jax
import jax.numpy as jnp
import numpy as np
from jax import lax
from jax.experimental import pallas as pl
from jax.experimental.pallas import tpu as pltpu
from jax.sharding import PartitionSpec as P

HEADS = 16
HEAD = 64


ALPHA = (3.0 * 200.0) ** 0.25
EPSILON = 1e-05
MASKED = -1e30


def rounded(values_in):
    return values_in.astype(jnp.bfloat16)


def product(first_side, other_side):
    return jnp.dot(first_side, other_side, preferred_element_type=jnp.float32)


def normalize(values_in, scale_row, shift_row):
    average = jnp.mean(values_in, axis=-1, keepdims=True)
    centred = values_in - average
    spread = jnp.mean(centred * centred, axis=-1, keepdims=True)
    return centred * lax.rsqrt(spread + EPSILON) * scale_row + shift_row


def normalize_back(values_in, scale_row, shift_row, grad_result):
    unused, pullback = jax.vjp(normalize, values_in, scale_row, shift_row)
    return pullback(grad_result)


def project_three(query_source, key_source, weight_stack):
    return (
        rounded(product(query_source, weight_stack[0])),
        rounded(product(key_source, weight_stack[1])),
        rounded(product(key_source, weight_stack[2])),
    )


def project_inputs(weight_stack, grad_query, grad_key, grad_value):
    grad_query_side = product(grad_query, weight_stack[0].T)
    grad_key_side = product(grad_key, weight_stack[1].T) + product(grad_value, weight_stack[2].T)
    return (grad_query_side, grad_key_side)


def masked_scores(head_query, head_key, allowed):
    scores = jnp.einsum(
        "qhd,khd->hqk", head_query, head_key, preferred_element_type=jnp.float32
    ) * HEAD ** (-0.5)
    return jnp.where(allowed[None], scores, MASKED)


def attend_forward(queries, key_rows, values, allowed):
    length = queries.shape[0]
    key_count = key_rows.shape[0]
    head_query = queries.reshape(length, HEADS, HEAD)
    head_key = key_rows.reshape(key_count, HEADS, HEAD)
    head_value = values.reshape(key_count, HEADS, HEAD)
    scores = masked_scores(head_query, head_key, allowed)
    largest = jnp.max(scores, axis=-1, keepdims=True)
    exponentials = jnp.exp(scores - largest)
    totals = jnp.sum(exponentials, axis=-1, keepdims=True)
    weights = rounded(exponentials / totals)
    mixed = jnp.einsum("hqk,khd->qhd", weights, head_value, preferred_element_type=jnp.float32)
    return (rounded(mixed.reshape(length, HEADS * HEAD)), largest + jnp.log(totals))


def attend_backward(queries, key_rows, values, allowed, logsum, grad_mixed):
    length = queries.shape[0]
    key_count = key_rows.shape[0]
    head_query = queries.reshape(length, HEADS, HEAD)
    head_key = key_rows.reshape(key_count, HEADS, HEAD)
    head_value = values.reshape(key_count, HEADS, HEAD)
    head_grad = grad_mixed.reshape(length, HEADS, HEAD)
    weights = jnp.exp(masked_scores(head_query, head_key, allowed) - logsum)
    grad_values = jnp.einsum(
        "hqk,qhd->khd", rounded(weights), head_grad, preferred_element_type=jnp.float32
    )
    grad_weights = jnp.einsum(
        "qhd,khd->hqk", head_grad, head_value, preferred_element_type=jnp.float32
    )
    inner_sum = jnp.sum(weights * grad_weights, axis=-1, keepdims=True)
    grad_scores = rounded(weights * (grad_weights - inner_sum))
    grad_queries = jnp.einsum(
        "hqk,khd->qhd", grad_scores, head_key, preferred_element_type=jnp.float32
    ) * HEAD ** (-0.5)
    grad_keys = jnp.einsum(
        "hqk,qhd->khd", grad_scores, head_query, preferred_element_type=jnp.float32
    ) * HEAD ** (-0.5)
    return (
        rounded(grad_queries.reshape(length, HEADS * HEAD)),
        rounded(grad_keys.reshape(key_count, HEADS * HEAD)),
        rounded(grad_values.reshape(key_count, HEADS * HEAD)),
    )


AXES = ("dp", "fsdp")


class Cube:
    def __init__(self, mesh):
        self.sizes = {axis: mesh.shape[axis] for axis in AXES}
        self.count = self.sizes["dp"] * self.sizes["fsdp"]
        inner = [("fsdp", k) for k in range(self.sizes["fsdp"].bit_length() - 1)]
        outer = [("dp", k) for k in range(self.sizes["dp"].bit_length() - 1)]
        self.place = {bit: k for k, bit in enumerate(inner + outer)}
        core, outer = outer[0], outer[1:]
        self.orders = {
            "A": [core, inner[0], *outer, *inner[1:]],
            "B": [core, *outer, *inner],
            "C": [core, inner[1], inner[0], *outer, *inner[2:]],
            "D": [core, inner[1], *outer, inner[0], *inner[2:]],
        }

    def index(self):
        return lax.axis_index("dp") * self.sizes["fsdp"] + lax.axis_index("fsdp")

    def swap(self, block, bit):
        axis, k = bit
        pairs = [(i, i ^ (1 << k)) for i in range(self.sizes[axis])]
        return lax.ppermute(block, axis, pairs)

    def offsets(self, name):
        order = self.orders[name]
        last = len(order) - 1
        return [
            sum(1 << self.place[bit] for k, bit in enumerate(order) if (p >> (last - k)) & 1)
            for p in range(self.count)
        ]

    def gather(self, shard, name):
        held = shard[None]
        for bit in self.orders[name][:0:-1]:
            held = jnp.concatenate([held, self.swap(held, bit)], axis=0)
        return held, self.swap(held, self.orders[name][0])

    def natural(self, halves, name):
        low, high = halves
        offsets = self.offsets(name)
        count, half = self.count, self.count // 2
        stack, rows, columns = low.shape[1:]
        if rows % 16:
            where = np.argsort(np.array(offsets))
            picked = jnp.asarray(where)[jnp.arange(count) ^ self.index()]
            blocks = jnp.take(jnp.concatenate(halves, axis=0), picked, axis=0)
            return blocks.transpose(1, 0, 2, 3).reshape(stack, count * rows, columns)

        def body(index_ref, low_ref, high_ref, out_ref, sems):
            index = index_ref[0]
            copies = []
            for p in range(count):
                source = low_ref.at[p] if p < half else high_ref.at[p - half]
                copies.append(pltpu.make_async_copy(source, out_ref.at[:, index ^ offsets[p]], sems.at[p]))
                copies[-1].start()
            for copy in copies:
                copy.wait()

        moved = pl.pallas_call(
            body,
            out_shape=jax.ShapeDtypeStruct((stack, count, rows, columns), low.dtype),
            in_specs=[
                pl.BlockSpec(memory_space=pltpu.SMEM),
                pl.BlockSpec(memory_space=pl.ANY),
                pl.BlockSpec(memory_space=pl.ANY),
            ],
            out_specs=pl.BlockSpec(memory_space=pltpu.VMEM),
            scratch_shapes=[pltpu.SemaphoreType.DMA((count,))],
            compiler_params=pltpu.CompilerParams(vmem_limit_bytes=40 * 2**20),
            name="natural_order",
        )(self.index().astype(jnp.int32).reshape(1), low, high)
        return moved.reshape(stack, count * rows, columns)

    def turned(self, values_in, names):
        tokens, features = values_in.shape
        count, rows = self.count, features // self.count
        tables = [self.offsets(name) for name in names]
        if rows % 16:
            blocks = values_in.T.reshape(count, rows, tokens)
            return [jnp.take(blocks, jnp.asarray(table) ^ self.index(), axis=0) for table in tables]

        def body(index_ref, in_ref, *refs):
            index = index_ref[0]
            outs, held = refs[:-1], refs[-1]
            held[...] = in_ref[...].T.reshape(count, rows, tokens)
            for table, out in zip(tables, outs):
                for p in range(count):
                    out[p] = held[index ^ table[p]]

        shape = (count, rows, tokens)
        return pl.pallas_call(
            body,
            out_shape=[jax.ShapeDtypeStruct(shape, values_in.dtype) for _ in tables],
            in_specs=[pl.BlockSpec(memory_space=pltpu.SMEM), pl.BlockSpec(memory_space=pltpu.VMEM)],
            out_specs=[pl.BlockSpec(memory_space=pltpu.VMEM) for _ in tables],
            scratch_shapes=[pltpu.VMEM(shape, values_in.dtype)],
            compiler_params=pltpu.CompilerParams(vmem_limit_bytes=40 * 2**20),
            name="turned",
        )(self.index().astype(jnp.int32).reshape(1), values_in)

    def scatter(self, turned, other_side, name):
        order = self.orders[name]
        count, rows, tokens = turned.shape
        half, quarter = count // 2, count // 4

        def part(first, last):
            return product(turned[first:last].reshape((last - first) * rows, tokens), other_side)

        got = self.swap(rounded(part(half, count)), order[0])
        sent = rounded(part(quarter, half) + got[quarter * rows :].astype(jnp.float32))
        kept = part(0, quarter) + got[: quarter * rows].astype(jnp.float32)
        for bit in order[1:-1]:
            got = self.swap(sent, bit).astype(jnp.float32)
            middle = kept.shape[0] // 2
            sent = rounded(kept[middle:] + got[middle:])
            kept = kept[:middle] + got[:middle]
        return kept + self.swap(sent, order[-1]).astype(jnp.float32)

    def scatter_small(self, rows_in):
        lines, features = rows_in.shape
        count = self.count
        own = features // count
        blocks = rows_in.reshape(lines, count, own).transpose(1, 0, 2)
        blocks = jnp.pad(blocks, ((0, 0), (0, 8 - lines), (0, 128 - own)))
        held = jnp.take(blocks, jnp.asarray(self.offsets("A")) ^ self.index(), axis=0)
        for bit in self.orders["A"]:
            middle = held.shape[0] // 2
            held = held[:middle] + self.swap(held[middle:], bit)
        return held[0, :lines, :own]

    def gather_small(self, rows_in):
        lines, own = rows_in.shape
        block = jnp.pad(rows_in, ((0, 16 - lines), (0, 128 - own)))
        held = jnp.concatenate(self.gather(block, "A"), axis=0)
        where = np.argsort(np.array(self.offsets("A")))
        picked = jnp.asarray(where)[jnp.arange(self.count) ^ self.index()]
        held = jnp.take(held, picked, axis=0)[:, :lines, :own]
        return held.transpose(1, 0, 2).reshape(lines, self.count * own)


def per_device(
    cube,
    tokens,
    memory,
    token_segments,
    memory_segments,
    padding,
    self_project,
    self_output,
    cross_project,
    cross_output,
    widen_weight,
    narrow_weight,
    norm_gain,
    norm_bias,
    grad_out,
):
    token_low = tokens[0]
    memory_low = memory[0]
    row_in = token_low.astype(jnp.float32)
    segment_row = token_segments[0]
    places = jnp.arange(segment_row.shape[0])
    diagonal = places[None, :] == places[:, None]
    live_keys = padding[0] == 1
    self_allowed = (
        (segment_row[:, None] == segment_row[None, :])
        & (places[None, :] <= places[:, None])
        & (live_keys[None, :] | diagonal)
    )
    cross_allowed = segment_row[:, None] == memory_segments[0][None, :]
    pad_scale = padding[0].astype(jnp.float32)[:, None]
    width = token_low.shape[1]
    own = self_project.shape[1]
    spread = widen_weight.shape[1] // width
    count = cube.count

    packed = jnp.concatenate(
        [
            cross_project.reshape(3 * own, width),
            cross_output,
            widen_weight.reshape(own, spread, width).transpose(1, 0, 2).reshape(spread * own, width),
            narrow_weight,
        ],
        axis=0,
    )
    later = lax.all_gather(packed, AXES, axis=0)
    first_pair = cube.natural(cube.gather(self_project[:2], "A"), "A")
    second_pair = cube.natural(
        cube.gather(jnp.concatenate([self_project[2:], self_output[None]], axis=0), "B"), "B"
    )
    self_stack = [first_pair[0], first_pair[1], second_pair[0]]
    self_final = second_pair[1]
    norms = cube.gather_small(jnp.concatenate([norm_gain, norm_bias], axis=0)).astype(jnp.float32)
    gain_values, bias_values = norms[:3], norms[3:]

    self_query, self_key, self_value = project_three(token_low, token_low, self_stack)
    self_mixed, self_logsum = attend_forward(self_query, self_key, self_value, self_allowed)
    pre_one = ALPHA * row_in + product(self_mixed, self_final)
    first_out = normalize(pre_one, gain_values[0], bias_values[0])
    first_low = rounded(first_out)

    cross_stack = [later[:, k * own : (k + 1) * own].reshape(width, width) for k in range(3)]
    cross_final = later[:, 3 * own : 4 * own].reshape(width, width)
    widen_full = (
        later[:, 4 * own : (4 + spread) * own]
        .reshape(count, spread, own, width)
        .transpose(0, 2, 1, 3)
        .reshape(width, spread * width)
    )
    narrow_full = later[:, (4 + spread) * own :].reshape(spread * width, width)

    cross_query, cross_key, cross_value = project_three(first_low, memory_low, cross_stack)
    cross_mixed, cross_logsum = attend_forward(cross_query, cross_key, cross_value, cross_allowed)
    pre_two = ALPHA * first_out + product(cross_mixed, cross_final)
    second = normalize(pre_two, gain_values[1], bias_values[1])
    second_low = rounded(second)

    hidden = product(second_low, widen_full)
    active = rounded(jax.nn.gelu(hidden))
    pre_three = ALPHA * second + product(active, narrow_full)
    third_out = normalize(pre_three, gain_values[2], bias_values[2])
    layer_out = rounded(third_out * pad_scale)

    token_turned = cube.turned(token_low, ["A", "B"])
    self_mixed_turned = cube.turned(self_mixed, ["D"])
    first_turned = cube.turned(first_low, ["D"])
    memory_turned = cube.turned(memory_low, ["B"])
    cross_mixed_turned = cube.turned(cross_mixed, ["B"])
    second_turned = cube.turned(second_low, ["C", "A"])
    active_turned = cube.turned(active, ["A", "B"])

    grad_third = grad_out[0].astype(jnp.float32) * pad_scale
    grad_pre_three, grad_gain_three, grad_bias_three = normalize_back(
        pre_three, gain_values[2], bias_values[2], grad_third
    )
    ffn_branch = rounded(grad_pre_three)
    middle = width // 2
    narrow_parts = [
        cube.scatter(active_turned[0], ffn_branch[:, :middle], "A"),
        cube.scatter(active_turned[1], ffn_branch[:, middle:], "B"),
    ]
    grad_active = product(ffn_branch, narrow_full.T)
    unused, gelu_pull = jax.vjp(jax.nn.gelu, hidden)
    grad_hidden = rounded(gelu_pull(grad_active)[0])
    middle = grad_hidden.shape[1] // 2
    widen_parts = [
        cube.scatter(second_turned[0], grad_hidden[:, :middle], "C"),
        cube.scatter(second_turned[1], grad_hidden[:, middle:], "A"),
    ]
    grad_second = ALPHA * grad_pre_three + product(grad_hidden, widen_full.T)

    grad_pre_two, grad_gain_two, grad_bias_two = normalize_back(
        pre_two, gain_values[1], bias_values[1], grad_second
    )
    cross_branch = rounded(grad_pre_two)
    grad_cross_final = cube.scatter(cross_mixed_turned[0], cross_branch, "B")
    grad_mixed = rounded(product(cross_branch, cross_final.T))
    cross_dq, cross_dk, cross_dv = attend_backward(
        cross_query, cross_key, cross_value, cross_allowed, cross_logsum, grad_mixed
    )
    grad_first_in, grad_memory = project_inputs(cross_stack, cross_dq, cross_dk, cross_dv)
    grad_first = ALPHA * grad_pre_two + grad_first_in
    cross_key_rows = cube.scatter(memory_turned[0], jnp.concatenate([cross_dk, cross_dv], axis=1), "B")
    cross_query_rows = cube.scatter(first_turned[0], cross_dq, "D")
    grad_cross_stack = jnp.stack([cross_query_rows, cross_key_rows[:, :width], cross_key_rows[:, width:]])

    grad_pre_one, grad_gain_one, grad_bias_one = normalize_back(
        pre_one, gain_values[0], bias_values[0], grad_first
    )
    self_branch = rounded(grad_pre_one)
    grad_self_final = cube.scatter(self_mixed_turned[0], self_branch, "D")
    grad_mixed = rounded(product(self_branch, self_final.T))
    self_dq, self_dk, self_dv = attend_backward(
        self_query, self_key, self_value, self_allowed, self_logsum, grad_mixed
    )
    grad_query_in, grad_key_in = project_inputs(self_stack, self_dq, self_dk, self_dv)
    grad_tokens = ALPHA * grad_pre_one + grad_query_in + grad_key_in
    self_value_rows = cube.scatter(token_turned[1], self_dv, "B")
    self_key_rows = cube.scatter(token_turned[0], jnp.concatenate([self_dq, self_dk], axis=1), "A")
    grad_self_stack = jnp.stack([self_key_rows[:, :width], self_key_rows[:, width:], self_value_rows])
    grad_norms = cube.scatter_small(
        jnp.stack(
            [
                grad_gain_one,
                grad_gain_two,
                grad_gain_three,
                grad_bias_one,
                grad_bias_two,
                grad_bias_three,
            ]
        )
    )
    return (
        layer_out[None],
        grad_tokens[None],
        grad_memory[None],
        grad_self_stack,
        grad_self_final,
        grad_cross_stack,
        grad_cross_final,
        jnp.concatenate(widen_parts, axis=1),
        jnp.concatenate(narrow_parts, axis=1),
        grad_norms[:3],
        grad_norms[3:],
    )


def solution(mesh):
    return jax.shard_map(
        functools.partial(per_device, Cube(mesh)),
        mesh=mesh,
        in_specs=(
            P(("dp", "fsdp"), None, None),
            P(("dp", "fsdp"), None, None),
            P(("dp", "fsdp"), None),
            P(("dp", "fsdp"), None),
            P(("dp", "fsdp"), None),
            P(None, ("dp", "fsdp"), None),
            P(("dp", "fsdp"), None),
            P(None, ("dp", "fsdp"), None),
            P(("dp", "fsdp"), None),
            P(("dp", "fsdp"), None),
            P(("dp", "fsdp"), None),
            P(None, ("dp", "fsdp")),
            P(None, ("dp", "fsdp")),
            P(("dp", "fsdp"), None, None),
        ),
        out_specs=(
            P(("dp", "fsdp"), None, None),
            P(("dp", "fsdp"), None, None),
            P(("dp", "fsdp"), None, None),
            P(None, ("dp", "fsdp"), None),
            P(("dp", "fsdp"), None),
            P(None, ("dp", "fsdp"), None),
            P(("dp", "fsdp"), None),
            P(("dp", "fsdp"), None),
            P(("dp", "fsdp"), None),
            P(None, ("dp", "fsdp")),
            P(None, ("dp", "fsdp")),
        ),
        check_vma=False,
    )
```

```python
import functools

import jax
import jax.numpy as jnp
import numpy as np
from jax import lax
from jax.experimental import pallas as pl
from jax.experimental.pallas import tpu as pltpu
from jax.sharding import PartitionSpec as P

HEADS = 16
HEAD = 64


ALPHA = (3.0 * 200.0) ** 0.25
EPSILON = 1e-05
MASKED = -1e30


def rounded(values_in):
    return values_in.astype(jnp.bfloat16)


def product(first_side, other_side):
    return jnp.dot(first_side, other_side, preferred_element_type=jnp.float32)


AXES = ("far", "pair", "core", "fsdp")
PAIR = ("pair", 0)
CORE = ("core", 0)
GATHER_DEPTH = 2
SCATTER_DEPTH = 2
GATHER = {"s1": "A", "s2": "B", "c1": "A", "c2": "B"}
SCATTER = {"N": "E", "W": "F", "P1": "B", "P2": "D", "S1": "A", "S2": "B"}
STEPS = {
    "start": [],
    "early": ["s1", "s2", "s1", "s2"],
    "self": ["c1", "c2", "s1", "s2", "c1", "c2", "widen", "s1", "s2", "c1", "c2", "s1", "s2"],
    "cross": ["c1", "c2", "narrow", "c1", "c2"],
    "gs": ["W", "N"],
    "gf": ["P2", "P1", "W", "N"],
    "tail": ["P2", "P1", "S1", "S2", "W", "N", "P2", "S1", "S2", "W", "N", "P1", "P2", "S1", "S2", "W", "P1", "P2", "S1", "S2", "P1", "S1", "S2"],
}


def normalize(values_in, scale_row, shift_row):
    average = jnp.mean(values_in, axis=-1, keepdims=True)
    centred = values_in - average
    spread = jnp.mean(centred * centred, axis=-1, keepdims=True)
    return centred * lax.rsqrt(spread + EPSILON) * scale_row + shift_row


def normalize_back(values_in, scale_row, shift_row, grad_result):
    unused, pullback = jax.vjp(normalize, values_in, scale_row, shift_row)
    return pullback(grad_result)


def project_three(query_source, key_source, weight_stack):
    return (
        rounded(product(query_source, weight_stack[0])),
        rounded(product(key_source, weight_stack[1])),
        rounded(product(key_source, weight_stack[2])),
    )


def project_inputs(weight_stack, grad_query, grad_key, grad_value):
    grad_query_side = product(grad_query, weight_stack[0].T)
    grad_key_side = product(grad_key, weight_stack[1].T) + product(grad_value, weight_stack[2].T)
    return (grad_query_side, grad_key_side)


def masked_scores(head_query, head_key, allowed):
    scores = jnp.einsum(
        "qhd,khd->hqk", head_query, head_key, preferred_element_type=jnp.float32
    ) * HEAD ** (-0.5)
    return jnp.where(allowed[None], scores, MASKED)


def attend_forward(queries, key_rows, values, allowed):
    length = queries.shape[0]
    key_count = key_rows.shape[0]
    head_query = queries.reshape(length, HEADS, HEAD)
    head_key = key_rows.reshape(key_count, HEADS, HEAD)
    head_value = values.reshape(key_count, HEADS, HEAD)
    scores = masked_scores(head_query, head_key, allowed)
    largest = jnp.max(scores, axis=-1, keepdims=True)
    exponentials = jnp.exp(scores - largest)
    totals = jnp.sum(exponentials, axis=-1, keepdims=True)
    weights = rounded(exponentials / totals)
    mixed = jnp.einsum("hqk,khd->qhd", weights, head_value, preferred_element_type=jnp.float32)
    return (rounded(mixed.reshape(length, HEADS * HEAD)), largest + jnp.log(totals))


def attend_backward(queries, key_rows, values, allowed, logsum, grad_mixed):
    length = queries.shape[0]
    key_count = key_rows.shape[0]
    head_query = queries.reshape(length, HEADS, HEAD)
    head_key = key_rows.reshape(key_count, HEADS, HEAD)
    head_value = values.reshape(key_count, HEADS, HEAD)
    head_grad = grad_mixed.reshape(length, HEADS, HEAD)
    weights = jnp.exp(masked_scores(head_query, head_key, allowed) - logsum)
    grad_values = jnp.einsum(
        "hqk,qhd->khd", rounded(weights), head_grad, preferred_element_type=jnp.float32
    )
    grad_weights = jnp.einsum(
        "qhd,khd->hqk", head_grad, head_value, preferred_element_type=jnp.float32
    )
    inner_sum = jnp.sum(weights * grad_weights, axis=-1, keepdims=True)
    grad_scores = rounded(weights * (grad_weights - inner_sum))
    grad_queries = jnp.einsum(
        "hqk,khd->qhd", grad_scores, head_key, preferred_element_type=jnp.float32
    ) * HEAD ** (-0.5)
    grad_keys = jnp.einsum(
        "hqk,qhd->khd", grad_scores, head_query, preferred_element_type=jnp.float32
    ) * HEAD ** (-0.5)
    return (
        rounded(grad_queries.reshape(length, HEADS * HEAD)),
        rounded(grad_keys.reshape(key_count, HEADS * HEAD)),
        rounded(grad_values.reshape(key_count, HEADS * HEAD)),
    )


class Cube:
    def __init__(self, mesh):
        far, inner = mesh.shape["dp"] // 4, mesh.shape["fsdp"]
        self.mesh = jax.sharding.Mesh(mesh.devices.reshape(far, 2, 2, inner), AXES)
        self.sizes = dict(zip(AXES, (far, 2, 2, inner)))
        self.count = 4 * far * inner
        self.far = far
        close = [("fsdp", k) for k in range(inner.bit_length() - 1)]
        apart = [("far", k) for k in range(far.bit_length() - 1)]
        self.place = {bit: k for k, bit in enumerate([*close, CORE, PAIR, *apart])}
        self.side_place = {bit: k for k, bit in enumerate([*close, CORE, *apart])}
        self.orders = {
            "A": [CORE, close[0], PAIR, *close[1:], *apart],
            "B": [CORE, PAIR, *close, *apart],
            "C": [CORE, close[1], close[0], PAIR, *close[2:], *apart],
            "D": [CORE, close[1], PAIR, close[0], *close[2:], *apart],
            "E": [CORE, *close, *apart],
            "F": [CORE, close[1], close[0], *close[2:], *apart],
        }

    def index(self, place):
        return sum(((lax.axis_index(axis) >> k) & 1) << shift for (axis, k), shift in place.items())

    def swap(self, block, bit):
        axis, k = bit
        return lax.ppermute(block, axis, [(i, i ^ (1 << k)) for i in range(self.sizes[axis])])

    def offsets(self, order, place):
        last = len(order) - 1
        return [
            sum(1 << place[bit] for k, bit in enumerate(order) if (p >> (last - k)) & 1)
            for p in range(1 << len(order))
        ]

    def gather(self, shard, order):
        held = shard[None]
        for bit in order[:0:-1]:
            held = jnp.concatenate([held, (yield held, bit)], axis=0)
        return held, (yield held, order[0])

    def natural(self, halves, order, segments):
        low, high = halves
        offsets = self.offsets(order, self.place)
        count, half = self.count, self.count // 2
        columns = low.shape[2]
        starts = [sum(segments[:k]) for k in range(len(segments))]
        if any(rows % 16 for rows in segments):
            where = np.argsort(np.array(offsets))
            picked = jnp.asarray(where)[jnp.arange(count) ^ self.index(self.place)]
            blocks = jnp.take(jnp.concatenate(halves, axis=0), picked, axis=0)
            return [
                blocks[:, start : start + rows].reshape(count * rows, columns)
                for start, rows in zip(starts, segments)
            ]
        pieces = list(enumerate(zip(starts, segments)))

        def body(index_ref, low_ref, high_ref, *refs):
            index, sems = index_ref[0], refs[-1]
            copies = []
            for p in range(count):
                source = low_ref.at[p] if p < half else high_ref.at[p - half]
                for k, (start, rows) in pieces:
                    copies.append(
                        pltpu.make_async_copy(
                            source.at[pl.ds(start, rows)], refs[k].at[index ^ offsets[p]], sems.at[p, k]
                        )
                    )
                    copies[-1].start()
            for copy in copies:
                copy.wait()

        moved = pl.pallas_call(
            body,
            out_shape=[jax.ShapeDtypeStruct((count, rows, columns), low.dtype) for rows in segments],
            in_specs=[
                pl.BlockSpec(memory_space=pltpu.SMEM),
                pl.BlockSpec(memory_space=pl.ANY),
                pl.BlockSpec(memory_space=pl.ANY),
            ],
            out_specs=[pl.BlockSpec(memory_space=pltpu.VMEM) for _ in segments],
            scratch_shapes=[pltpu.SemaphoreType.DMA((count, len(segments)))],
            compiler_params=pltpu.CompilerParams(vmem_limit_bytes=40 * 2**20),
            name="natural_order",
        )(self.index(self.place).astype(jnp.int32).reshape(1), low, high)
        return [block.reshape(count * rows, columns) for block, rows in zip(moved, segments)]

    def turned(self, sources, orders, place):
        tokens, features = sources[0].shape
        count = 1 << len(place)
        rows, wide = features // count, tokens * len(sources)
        tables = [self.offsets(order, place) for order in orders]
        index = self.index(place)
        if rows % 16:
            blocks = jnp.concatenate(sources, axis=0).T.reshape(count, rows, wide)
            return [jnp.take(blocks, jnp.asarray(table) ^ index, axis=0) for table in tables]

        def body(index_ref, *refs):
            index = index_ref[0]
            ins, outs, held = refs[: len(sources)], refs[len(sources) : -1], refs[-1]
            for k, in_ref in enumerate(ins):
                held[:, :, pl.ds(k * tokens, tokens)] = in_ref[...].T.reshape(count, rows, tokens)
            for table, out in zip(tables, outs):
                for p in range(count):
                    out[p] = held[index ^ table[p]]

        shape = (count, rows, wide)
        return pl.pallas_call(
            body,
            out_shape=[jax.ShapeDtypeStruct(shape, sources[0].dtype) for _ in tables],
            in_specs=[pl.BlockSpec(memory_space=pltpu.SMEM)]
            + [pl.BlockSpec(memory_space=pltpu.VMEM) for _ in sources],
            out_specs=[pl.BlockSpec(memory_space=pltpu.VMEM) for _ in tables],
            scratch_shapes=[pltpu.VMEM(shape, sources[0].dtype)],
            compiler_params=pltpu.CompilerParams(vmem_limit_bytes=40 * 2**20),
            name="turned",
        )(index.astype(jnp.int32).reshape(1), *sources)

    def scatter(self, sides, order, extra=None):
        blocks = 1 << len(order)
        half, quarter = blocks // 2, blocks // 4

        def parts(first, last, got=None):
            terms, column = [], 0
            for turned, other in sides:
                rows = turned.shape[0] // blocks
                block = turned[first * rows : last * rows]
                term = product(block.reshape(-1, turned.shape[-1]), other)
                if got is not None:
                    term = term + got[:, column : column + term.shape[1]].astype(jnp.float32)
                column += term.shape[1]
                terms.append(term)
            if extra is not None:
                rows = extra.shape[0] // blocks
                term = extra[first * rows : last * rows]
                if got is not None:
                    term = term + got[:, column:].astype(jnp.float32)
                terms.append(term)
            return terms

        def joined(terms):
            return terms[0] if len(terms) == 1 else jnp.concatenate(terms, axis=1)

        got = yield joined([rounded(term) for term in parts(half, blocks)]), order[0]
        middle = got.shape[0] // 2
        sent = joined([rounded(term) for term in parts(quarter, half, got[middle:])])
        kept = joined(parts(0, quarter, got[:middle]))
        for bit in order[1:-1]:
            got = yield sent, bit
            middle = kept.shape[0] // 2
            sent = rounded(kept[middle:] + got[middle:].astype(jnp.float32))
            kept = kept[:middle] + got[:middle].astype(jnp.float32)
        return kept + (yield sent, order[-1]).astype(jnp.float32)

    def scatter_pair(self, sides, order):
        kept = yield from self.scatter(sides, order)
        middle = kept.shape[0] // 2
        got = (yield rounded(kept[middle:]), PAIR).astype(jnp.float32)
        return kept[:middle], got


    def columns(self, vectors, order):
        lines, features = vectors.shape
        own = features // self.count
        blocks = jnp.pad(vectors.T, ((0, 0), (0, 128 - lines))).reshape(self.count, own, 128)
        table = jnp.asarray(self.offsets(order, self.place))
        return jnp.take(blocks, table ^ self.index(self.place), axis=0).reshape(features, 128)


class Driver:
    def __init__(self, cube, depth):
        self.cube, self.depth = cube, depth
        self.before = {bit: [] for bit in cube.place}
        self.chains, self.got, self.results = {}, {}, {}
        self.token = None
        self.hooks = {}

    def swap(self, block, bit):
        past = self.before[bit]
        if len(past) >= self.depth:
            block, _ = lax.optimization_barrier((block, past[-self.depth]))
        past.append(self.cube.swap(block, bit))
        return past[-1]

    def after(self, block):
        if self.token is None:
            return block
        return lax.optimization_barrier((block, self.token))[0]

    def done(self, block):
        self.token = block
        return block

    def add(self, name, chain):
        self.chains[name] = chain
        block, bit = next(chain)
        self.token = block
        self.got[name] = self.swap(block, bit)

    def advance(self, names):
        for name in names:
            if name in self.hooks:
                self.results[name] = self.hooks.pop(name)()
            if name in self.results:
                continue
            got = self.after(self.got[name])
            try:
                block, bit = self.chains[name].send(got)
            except StopIteration as stop:
                self.results[name] = stop.value
                continue
            self.token = block
            self.got[name] = self.swap(block, bit)

    def finish(self, names):
        while left := [name for name in names if name not in self.results]:
            self.advance(left)
        return [self.results[name] for name in names]


def per_device(
    cube,
    tokens,
    memory,
    token_segments,
    memory_segments,
    padding,
    self_project,
    self_output,
    cross_project,
    cross_output,
    widen_weight,
    narrow_weight,
    norm_gain,
    norm_bias,
    grad_out,
):
    token_low = tokens[0]
    memory_low = memory[0]
    row_in = token_low.astype(jnp.float32)
    segment_row = token_segments[0]
    places = jnp.arange(segment_row.shape[0])
    diagonal = places[None, :] == places[:, None]
    live_keys = padding[0] == 1
    self_allowed = (
        (segment_row[:, None] == segment_row[None, :])
        & (places[None, :] <= places[:, None])
        & (live_keys[None, :] | diagonal)
    )
    cross_allowed = segment_row[:, None] == memory_segments[0][None, :]
    pad_scale = padding[0].astype(jnp.float32)[:, None]
    width = token_low.shape[1]
    own = self_project.shape[1]
    hidden_width = widen_weight.shape[1]
    count, far = cube.count, cube.far
    orders = cube.orders
    side = lax.axis_index("pair")
    drive = Driver(cube, GATHER_DEPTH)

    def both_sides(mine, other):
        return [jnp.where(side == 0, mine, other), jnp.where(side == 0, other, mine)]

    shard = widen_weight.reshape(own, far, 2, hidden_width // (2 * far))
    mine, other = (
        lax.dynamic_index_in_dim(shard, k, axis=2, keepdims=False).reshape(own, hidden_width // 2)
        for k in (side, 1 - side)
    )
    widen_shard = jnp.stack(both_sides(mine, drive.swap(other, PAIR)))

    def gather_widen():
        full = lax.all_gather(drive.after(widen_shard), ("far", "core", "fsdp"), axis=1, tiled=True)
        return (
            full.reshape(2, far, width // (2 * far), hidden_width // 2)
            .transpose(1, 0, 2, 3)
            .reshape(width, hidden_width // 2)
        )

    def gather_narrow():
        return lax.all_gather(drive.after(narrow_weight), ("far", "core", "fsdp"), axis=0, tiled=True)

    drive.hooks = {"widen": gather_widen, "narrow": gather_narrow}
    drive.advance(STEPS["start"])
    norm_rows = jnp.concatenate([norm_gain, norm_bias], axis=0)
    norm_rows = jnp.pad(norm_rows, ((0, 16 - 6), (0, width - own)))
    drive.add("s1", cube.gather(self_project[:2].reshape(2 * own, width), orders[GATHER["s1"]]))
    drive.add(
        "s2",
        cube.gather(
            jnp.concatenate([self_project[2], self_output, norm_rows], axis=0), orders[GATHER["s2"]]
        ),
    )
    drive.advance(STEPS["early"])
    drive.add("c1", cube.gather(cross_project[:2].reshape(2 * own, width), orders[GATHER["c1"]]))
    drive.add(
        "c2",
        cube.gather(jnp.concatenate([cross_project[2], cross_output], axis=0), orders[GATHER["c2"]]),
    )
    drive.advance(STEPS["self"])
    drive.finish(["s1", "s2"])
    query_full, key_full = cube.natural(drive.results["s1"], orders[GATHER["s1"]], [own, own])
    value_full, self_final, norms = cube.natural(drive.results["s2"], orders[GATHER["s2"]], [own, own, 16])
    self_stack = [query_full, key_full, value_full]
    norms = norms.reshape(count, 16, width)[:, :6, :own].transpose(1, 0, 2).reshape(6, width)
    norms = norms.astype(jnp.float32)
    gain_values, bias_values = norms[:3], norms[3:]

    self_query, self_key, self_value = project_three(token_low, token_low, self_stack)
    self_mixed, self_logsum = attend_forward(self_query, self_key, self_value, self_allowed)
    pre_one = ALPHA * row_in + product(self_mixed, self_final)
    first_out = normalize(pre_one, gain_values[0], bias_values[0])
    first_low = rounded(first_out)

    drive.done(first_low)
    drive.advance(STEPS["cross"])
    drive.finish(["c1", "c2"])
    widen_full, narrow_full = drive.finish(["widen", "narrow"])
    query_full, key_full = cube.natural(drive.results["c1"], orders[GATHER["c1"]], [own, own])
    value_full, cross_final = cube.natural(drive.results["c2"], orders[GATHER["c2"]], [own, own])
    cross_stack = [query_full, key_full, value_full]
    cross_query, cross_key, cross_value = project_three(first_low, memory_low, cross_stack)
    cross_mixed, cross_logsum = attend_forward(cross_query, cross_key, cross_value, cross_allowed)
    pre_two = ALPHA * first_out + product(cross_mixed, cross_final)
    second = normalize(pre_two, gain_values[1], bias_values[1])
    second_low = rounded(second)

    def widened(rows_low):
        hidden = product(rows_low, widen_full)
        active = rounded(jax.nn.gelu(hidden))
        return hidden, active, product(active, narrow_full)

    second_other = cube.swap(second_low, PAIR)
    hidden, active, branch = widened(second_low)
    hidden_other, active_other, branch_other = widened(second_other)
    branch_got = cube.swap(rounded(branch_other), PAIR)
    pre_three = ALPHA * second + (branch + branch_got.astype(jnp.float32))
    third_out = normalize(pre_three, gain_values[2], bias_values[2])
    layer_out = rounded(third_out * pad_scale)

    (self_mixed_turned,) = cube.turned([self_mixed], [orders[SCATTER["S2"]]], cube.place)
    token_turned = cube.turned([token_low], [orders[SCATTER["S1"]], orders[SCATTER["S2"]]], cube.place)
    (first_turned,) = cube.turned([first_low], [orders[SCATTER["P2"]]], cube.place)
    (memory_turned,) = cube.turned([memory_low], [orders[SCATTER["P1"]]], cube.place)
    (cross_mixed_turned,) = cube.turned([cross_mixed], [orders[SCATTER["P2"]]], cube.place)
    (second_turned,) = cube.turned([second_low, second_other], [[*orders[SCATTER["W"]], PAIR]], cube.place)
    (active_turned,) = cube.turned([active, active_other], [orders[SCATTER["N"]]], cube.side_place)
    drive = Driver(cube, SCATTER_DEPTH)

    grad_third = grad_out[0].astype(jnp.float32) * pad_scale
    grad_pre_three, grad_gain_three, grad_bias_three = normalize_back(
        pre_three, gain_values[2], bias_values[2], grad_third
    )
    ffn_branch = rounded(grad_pre_three)

    def widened_back(branch_low, hidden):
        grad_active = product(branch_low, narrow_full.T)
        unused, gelu_pull = jax.vjp(jax.nn.gelu, hidden)
        grad_hidden = rounded(gelu_pull(grad_active)[0])
        return grad_hidden, product(grad_hidden, widen_full.T)

    ffn_branch_other = cube.swap(ffn_branch, PAIR)
    grad_hidden, grad_branch = widened_back(ffn_branch, hidden)
    grad_hidden_other, grad_branch_other = widened_back(ffn_branch_other, hidden_other)
    grad_branch_got = drive.swap(drive.done(rounded(grad_branch_other)), PAIR)
    drive.add(
        "N",
        cube.scatter(
            [(drive.after(active_turned), jnp.concatenate([ffn_branch, ffn_branch_other], axis=0))], orders[SCATTER["N"]]
        ),
    )
    drive.add(
        "W",
        cube.scatter_pair(
            [(drive.after(second_turned), jnp.concatenate([grad_hidden, grad_hidden_other], axis=0))],
            orders[SCATTER["W"]],
        ),
    )
    grad_branch_got = drive.after(grad_branch_got)
    grad_second = ALPHA * grad_pre_three + (grad_branch + grad_branch_got.astype(jnp.float32))

    grad_pre_two, grad_gain_two, grad_bias_two = normalize_back(
        pre_two, gain_values[1], bias_values[1], grad_second
    )
    cross_branch = drive.done(rounded(grad_pre_two))
    drive.advance(STEPS["gs"])
    cross_branch = drive.after(cross_branch)
    grad_mixed = rounded(product(cross_branch, cross_final.T))
    cross_dq, cross_dk, cross_dv = attend_backward(
        cross_query, cross_key, cross_value, cross_allowed, cross_logsum, grad_mixed
    )
    grad_first_in, grad_memory = project_inputs(cross_stack, cross_dq, cross_dk, cross_dv)
    grad_first = ALPHA * grad_pre_two + grad_first_in
    drive.add(
        "P1",
        cube.scatter([(memory_turned, jnp.concatenate([cross_dk, cross_dv], axis=1))], orders[SCATTER["P1"]]),
    )
    drive.add(
        "P2",
        cube.scatter([(first_turned, cross_dq), (cross_mixed_turned, cross_branch)], orders[SCATTER["P2"]]),
    )
    drive.advance(STEPS["gf"])
    grad_first = drive.after(grad_first)

    grad_pre_one, grad_gain_one, grad_bias_one = normalize_back(
        pre_one, gain_values[0], bias_values[0], grad_first
    )
    self_branch = rounded(grad_pre_one)
    grad_mixed = rounded(product(self_branch, self_final.T))
    self_dq, self_dk, self_dv = attend_backward(
        self_query, self_key, self_value, self_allowed, self_logsum, grad_mixed
    )
    grad_query_in, grad_key_in = project_inputs(self_stack, self_dq, self_dk, self_dv)
    grad_tokens = ALPHA * grad_pre_one + grad_query_in + grad_key_in
    grad_norms = lax.optimization_barrier(
        jnp.stack(
            [
                grad_gain_one,
                grad_gain_two,
                grad_gain_three,
                grad_bias_one,
                grad_bias_two,
                grad_bias_three,
            ]
        )
    )
    drive.add(
        "S1",
        cube.scatter(
            [(token_turned[0], jnp.concatenate([self_dq, self_dk], axis=1))], orders[SCATTER["S1"]]
        ),
    )
    drive.add(
        "S2",
        cube.scatter(
            [(token_turned[1], self_dv), (self_mixed_turned, self_branch)],
            orders[SCATTER["S2"]],
            cube.columns(grad_norms, orders[SCATTER["S2"]]),
        ),
    )
    drive.advance(STEPS["tail"])
    drive.finish(["N", "W", "P1", "P2", "S1", "S2"])
    sums = drive.results
    grad_norms = sums["S2"][:, 2 * width : 2 * width + 6].T
    widen_mine, widen_other = sums["W"]
    grad_widen = jnp.stack(
        [
            block.reshape(own, far, hidden_width // (2 * far))
            for block in both_sides(widen_mine, widen_other)
        ],
        axis=2,
    ).reshape(own, hidden_width)
    return (
        layer_out[None],
        grad_tokens[None],
        grad_memory[None],
        jnp.stack([sums["S1"][:, :width], sums["S1"][:, width:], sums["S2"][:, :width]]),
        sums["S2"][:, width : 2 * width],
        jnp.stack([sums["P2"][:, :width], sums["P1"][:, :width], sums["P1"][:, width:]]),
        sums["P2"][:, width:],
        grad_widen,
        sums["N"],
        grad_norms[:3],
        grad_norms[3:],
    )


def solution(mesh):
    cube = Cube(mesh)
    return jax.shard_map(
        functools.partial(per_device, cube),
        mesh=cube.mesh,
        in_specs=(
            P(AXES, None, None),
            P(AXES, None, None),
            P(AXES, None),
            P(AXES, None),
            P(AXES, None),
            P(None, AXES, None),
            P(AXES, None),
            P(None, AXES, None),
            P(AXES, None),
            P(AXES, None),
            P(AXES, None),
            P(None, AXES),
            P(None, AXES),
            P(AXES, None, None),
        ),
        out_specs=(
            P(AXES, None, None),
            P(AXES, None, None),
            P(AXES, None, None),
            P(None, AXES, None),
            P(AXES, None),
            P(None, AXES, None),
            P(AXES, None),
            P(AXES, None),
            P(AXES, None),
            P(None, AXES),
            P(None, AXES),
        ),
        check_vma=False,
    )
```

```python
import functools

import jax
import jax.numpy as jnp
import numpy as np
from jax import lax
from jax.experimental import pallas as pl
from jax.experimental.pallas import tpu as pltpu
from jax.sharding import PartitionSpec as P

HEADS = 16
HEAD = 64


ALPHA = (3.0 * 200.0) ** 0.25
EPSILON = 1e-05
MASKED = -1e30


def rounded(values_in):
    return values_in.astype(jnp.bfloat16)


def product(first_side, other_side):
    return jnp.dot(first_side, other_side, preferred_element_type=jnp.float32)


AXES = ("far", "pair", "core", "fsdp")
PAIR = ("pair", 0)
CORE = ("core", 0)
GATHER_DEPTH = 2
SCATTER_DEPTH = 2
GATHER = {"s1": "A", "s2": "B", "c1": "A", "c2": "B"}
SCATTER = {"N": "E", "W": "F", "P1": "B", "P2": "D", "S1": "A", "S2": "B"}
STEPS = {
    "gs": ["W", "N"],
    "gf": ["P2", "P1", "W", "N"],
    "pre": [],
    "tail": ["P2", "P1", "S1", "S2", "W", "N", "P2", "P1", "S1", "S2", "W", "N", "P2", "P1", "S2", "S1", "W", "P2", "P1", "S2", "S1", "S2", "S1"],
    "early": ["s", "cross", "s", "c", "s", "s1", "s2", "c"],
    "self": ["s1", "s2", "c", "wide", "c1", "c2", "s1", "s2", "c1", "c2", "s1", "s2"],
    "cross": ["c1", "c2", "c1", "c2"],
}


def normalize(values_in, scale_row, shift_row):
    average = jnp.mean(values_in, axis=-1, keepdims=True)
    centred = values_in - average
    spread = jnp.mean(centred * centred, axis=-1, keepdims=True)
    return centred * lax.rsqrt(spread + EPSILON) * scale_row + shift_row


def normalize_back(values_in, scale_row, shift_row, grad_result):
    unused, pullback = jax.vjp(normalize, values_in, scale_row, shift_row)
    return pullback(grad_result)


def project_three(query_source, key_source, weight_stack):
    return (
        rounded(product(query_source, weight_stack[0])),
        rounded(product(key_source, weight_stack[1])),
        rounded(product(key_source, weight_stack[2])),
    )


def project_inputs(weight_stack, grad_query, grad_key, grad_value):
    grad_query_side = product(grad_query, weight_stack[0].T)
    grad_key_side = product(grad_key, weight_stack[1].T) + product(grad_value, weight_stack[2].T)
    return (grad_query_side, grad_key_side)


def masked_scores(head_query, head_key, allowed):
    scores = jnp.einsum(
        "qhd,khd->hqk", head_query, head_key, preferred_element_type=jnp.float32
    ) * HEAD ** (-0.5)
    return jnp.where(allowed[None], scores, MASKED)


def attend_forward(queries, key_rows, values, allowed):
    length = queries.shape[0]
    key_count = key_rows.shape[0]
    head_query = queries.reshape(length, HEADS, HEAD)
    head_key = key_rows.reshape(key_count, HEADS, HEAD)
    head_value = values.reshape(key_count, HEADS, HEAD)
    scores = masked_scores(head_query, head_key, allowed)
    largest = jnp.max(scores, axis=-1, keepdims=True)
    exponentials = jnp.exp(scores - largest)
    totals = jnp.sum(exponentials, axis=-1, keepdims=True)
    weights = rounded(exponentials / totals)
    mixed = jnp.einsum("hqk,khd->qhd", weights, head_value, preferred_element_type=jnp.float32)
    return (rounded(mixed.reshape(length, HEADS * HEAD)), largest + jnp.log(totals))


def attend_backward(queries, key_rows, values, allowed, logsum, grad_mixed):
    length = queries.shape[0]
    key_count = key_rows.shape[0]
    head_query = queries.reshape(length, HEADS, HEAD)
    head_key = key_rows.reshape(key_count, HEADS, HEAD)
    head_value = values.reshape(key_count, HEADS, HEAD)
    head_grad = grad_mixed.reshape(length, HEADS, HEAD)
    weights = jnp.exp(masked_scores(head_query, head_key, allowed) - logsum)
    grad_values = jnp.einsum(
        "hqk,qhd->khd", rounded(weights), head_grad, preferred_element_type=jnp.float32
    )
    grad_weights = jnp.einsum(
        "qhd,khd->hqk", head_grad, head_value, preferred_element_type=jnp.float32
    )
    inner_sum = jnp.sum(weights * grad_weights, axis=-1, keepdims=True)
    grad_scores = rounded(weights * (grad_weights - inner_sum))
    grad_queries = jnp.einsum(
        "hqk,khd->qhd", grad_scores, head_key, preferred_element_type=jnp.float32
    ) * HEAD ** (-0.5)
    grad_keys = jnp.einsum(
        "hqk,qhd->khd", grad_scores, head_query, preferred_element_type=jnp.float32
    ) * HEAD ** (-0.5)
    return (
        rounded(grad_queries.reshape(length, HEADS * HEAD)),
        rounded(grad_keys.reshape(key_count, HEADS * HEAD)),
        rounded(grad_values.reshape(key_count, HEADS * HEAD)),
    )


class Cube:
    def __init__(self, mesh):
        far, inner = mesh.shape["dp"] // 4, mesh.shape["fsdp"]
        self.mesh = jax.sharding.Mesh(mesh.devices.reshape(far, 2, 2, inner), AXES)
        self.sizes = dict(zip(AXES, (far, 2, 2, inner)))
        self.count = 4 * far * inner
        self.far = far
        close = [("fsdp", k) for k in range(inner.bit_length() - 1)]
        apart = [("far", k) for k in range(far.bit_length() - 1)]
        self.place = {bit: k for k, bit in enumerate([*close, CORE, PAIR, *apart])}
        self.side_place = {bit: k for k, bit in enumerate([*close, CORE, *apart])}
        self.orders = {
            "A": [CORE, close[0], PAIR, *close[1:], *apart],
            "B": [CORE, PAIR, *close, *apart],
            "C": [CORE, close[1], close[0], PAIR, *close[2:], *apart],
            "D": [CORE, close[1], PAIR, close[0], *close[2:], *apart],
            "E": [CORE, *close, *apart],
            "F": [CORE, close[1], close[0], *close[2:], *apart],
            "H": [CORE, *close[1:], close[0], *apart],
        }

    def index(self, place):
        return sum(((lax.axis_index(axis) >> k) & 1) << shift for (axis, k), shift in place.items())

    def swap(self, block, bit):
        axis, k = bit
        return lax.ppermute(block, axis, [(i, i ^ (1 << k)) for i in range(self.sizes[axis])])

    def offsets(self, order, place):
        last = len(order) - 1
        return [
            sum(1 << place[bit] for k, bit in enumerate(order) if (p >> (last - k)) & 1)
            for p in range(1 << len(order))
        ]

    def spread(self, held, bits):
        for bit in bits:
            held = jnp.concatenate([held, (yield held, bit)], axis=0)
        return held

    def gather(self, held, order):
        done = held.shape[0].bit_length() - 1
        held = yield from self.spread(held, order[:0:-1][done:])
        return held, (yield held, order[0])

    def natural(self, halves, order, segments, place):
        low, high = halves
        offsets = self.offsets(order, place)
        count, half = 2 * low.shape[0], low.shape[0]
        columns = low.shape[2]
        starts = [sum(segments[:k]) for k in range(len(segments))]
        index = self.index(place)
        if any(rows % 16 for rows in segments):
            where = np.argsort(np.array(offsets))
            picked = jnp.asarray(where)[jnp.arange(count) ^ index]
            blocks = jnp.take(jnp.concatenate(halves, axis=0), picked, axis=0)
            return [
                blocks[:, start : start + rows].reshape(count * rows, columns)
                for start, rows in zip(starts, segments)
            ]
        pieces = list(enumerate(zip(starts, segments)))

        def body(index_ref, low_ref, high_ref, *refs):
            index, sems = index_ref[0], refs[-1]
            copies = []
            for p in range(count):
                source = low_ref.at[p] if p < half else high_ref.at[p - half]
                for k, (start, rows) in pieces:
                    copies.append(
                        pltpu.make_async_copy(
                            source.at[pl.ds(start, rows)], refs[k].at[index ^ offsets[p]], sems.at[p, k]
                        )
                    )
                    copies[-1].start()
            for copy in copies:
                copy.wait()

        moved = pl.pallas_call(
            body,
            out_shape=[jax.ShapeDtypeStruct((count, rows, columns), low.dtype) for rows in segments],
            in_specs=[
                pl.BlockSpec(memory_space=pltpu.SMEM),
                pl.BlockSpec(memory_space=pl.ANY),
                pl.BlockSpec(memory_space=pl.ANY),
            ],
            out_specs=[pl.BlockSpec(memory_space=pltpu.VMEM) for _ in segments],
            scratch_shapes=[pltpu.SemaphoreType.DMA((count, len(segments)))],
            compiler_params=pltpu.CompilerParams(vmem_limit_bytes=40 * 2**20),
            name="natural_order",
        )(index.astype(jnp.int32).reshape(1), low, high)
        return [block.reshape(count * rows, columns) for block, rows in zip(moved, segments)]

    def unpacked(self, packed):
        rows, columns = packed.shape[1] // (self.count // 2), packed.shape[2]
        count, far, half = self.count // 2, self.far, columns // 2

        def widen(blocks):
            return blocks.reshape(2, far, -1, columns).transpose(1, 0, 2, 3).reshape(-1, columns)

        if rows % 16:
            narrow = packed[2:].reshape(2, count, rows, 2, half).transpose(1, 3, 0, 2, 4)
            return widen(packed[:2]), narrow.reshape(-1, half)

        def body(packed_ref, widen_ref, narrow_ref, sems):
            copies = [pltpu.make_async_copy(packed_ref.at[pl.ds(0, 2)], widen_ref, sems.at[0])]
            for p in range(count):
                for k in range(4):
                    source = packed_ref.at[
                        2 + k % 2, pl.ds(p * rows, rows), pl.ds((k // 2) * half, half)
                    ]
                    copies.append(
                        pltpu.make_async_copy(
                            source, narrow_ref.at[p, pl.ds(k * rows, rows)], sems.at[1 + 4 * p + k]
                        )
                    )
            for copy in copies:
                copy.start()
            for copy in copies:
                copy.wait()

        wide, narrow = pl.pallas_call(
            body,
            out_shape=[
                jax.ShapeDtypeStruct((2, count * rows, columns), packed.dtype),
                jax.ShapeDtypeStruct((count, 4 * rows, half), packed.dtype),
            ],
            in_specs=[pl.BlockSpec(memory_space=pl.ANY)],
            out_specs=[pl.BlockSpec(memory_space=pltpu.VMEM)] * 2,
            scratch_shapes=[pltpu.SemaphoreType.DMA((1 + 4 * count,))],
            compiler_params=pltpu.CompilerParams(vmem_limit_bytes=40 * 2**20),
            name="unpacked",
        )(packed)
        return widen(wide), narrow.reshape(-1, half)

    def turned(self, sources, orders, place):
        tokens, features = sources[0].shape
        count = 1 << len(place)
        rows, wide = features // count, tokens * len(sources)
        tables = [self.offsets(order, place) for order in orders]
        index = self.index(place)
        if rows % 16:
            blocks = jnp.concatenate(sources, axis=0).T.reshape(count, rows, wide)
            return [jnp.take(blocks, jnp.asarray(table) ^ index, axis=0) for table in tables]

        def body(index_ref, *refs):
            index = index_ref[0]
            ins, outs, held = refs[: len(sources)], refs[len(sources) : -1], refs[-1]
            for k, in_ref in enumerate(ins):
                held[:, :, pl.ds(k * tokens, tokens)] = in_ref[...].T.reshape(count, rows, tokens)
            for table, out in zip(tables, outs):
                for p in range(count):
                    out[p] = held[index ^ table[p]]

        shape = (count, rows, wide)
        return pl.pallas_call(
            body,
            out_shape=[jax.ShapeDtypeStruct(shape, sources[0].dtype) for _ in tables],
            in_specs=[pl.BlockSpec(memory_space=pltpu.SMEM)]
            + [pl.BlockSpec(memory_space=pltpu.VMEM) for _ in sources],
            out_specs=[pl.BlockSpec(memory_space=pltpu.VMEM) for _ in tables],
            scratch_shapes=[pltpu.VMEM(shape, sources[0].dtype)],
            compiler_params=pltpu.CompilerParams(vmem_limit_bytes=40 * 2**20),
            name="turned",
        )(index.astype(jnp.int32).reshape(1), *sources)

    def scatter(self, sides, order, extra=None):
        blocks = 1 << len(order)
        half, quarter = blocks // 2, blocks // 4

        def parts(first, last, got=None):
            terms, column = [], 0
            for turned, other in sides:
                rows = turned.shape[0] // blocks
                block = turned[first * rows : last * rows]
                term = product(block.reshape(-1, turned.shape[-1]), other)
                if got is not None:
                    term = term + got[:, column : column + term.shape[1]].astype(jnp.float32)
                column += term.shape[1]
                terms.append(term)
            if extra is not None:
                rows = extra.shape[0] // blocks
                term = extra[first * rows : last * rows]
                if got is not None:
                    term = term + got[:, column:].astype(jnp.float32)
                terms.append(term)
            return terms

        def joined(terms):
            return terms[0] if len(terms) == 1 else jnp.concatenate(terms, axis=1)

        got = yield joined([rounded(term) for term in parts(half, blocks)]), order[0]
        middle = got.shape[0] // 2
        sent = joined([rounded(term) for term in parts(quarter, half, got[middle:])])
        kept = joined(parts(0, quarter, got[:middle]))
        for bit in order[1:-1]:
            got = yield sent, bit
            middle = kept.shape[0] // 2
            sent = rounded(kept[middle:] + got[middle:].astype(jnp.float32))
            kept = kept[:middle] + got[:middle].astype(jnp.float32)
        return kept + (yield sent, order[-1]).astype(jnp.float32)

    def scatter_pair(self, sides, order):
        kept = yield from self.scatter(sides, order)
        middle = kept.shape[0] // 2
        got = (yield rounded(kept[middle:]), PAIR).astype(jnp.float32)
        return kept[:middle], got


    def columns(self, vectors, order):
        lines, features = vectors.shape
        own = features // self.count
        blocks = jnp.pad(vectors.T, ((0, 0), (0, 128 - lines))).reshape(self.count, own, 128)
        table = jnp.asarray(self.offsets(order, self.place))
        return jnp.take(blocks, table ^ self.index(self.place), axis=0).reshape(features, 128)


class Driver:
    def __init__(self, cube, depth):
        self.cube, self.depth = cube, depth
        self.before = {bit: [] for bit in cube.place}
        self.chains, self.got, self.results = {}, {}, {}
        self.token = None
        self.starts, self.calls = {}, {}

    def swap(self, block, bit):
        past = self.before[bit]
        if len(past) >= self.depth:
            block, _ = lax.optimization_barrier((block, past[-self.depth]))
        past.append(self.cube.swap(block, bit))
        return past[-1]

    def after(self, block):
        if self.token is None:
            return block
        return lax.optimization_barrier((block, self.token))[0]

    def done(self, block):
        self.token = block
        return block

    def add(self, name, chain):
        self.chains[name] = chain
        block, bit = next(chain)
        self.token = block
        self.got[name] = self.swap(block, bit)

    def advance(self, names):
        for name in names:
            if name in self.calls:
                self.results[name] = self.calls.pop(name)()
                continue
            if name in self.starts:
                self.add(name, self.starts.pop(name)())
                continue
            if name in self.results:
                continue
            got = self.after(self.got[name])
            try:
                block, bit = self.chains[name].send(got)
            except StopIteration as stop:
                self.results[name] = stop.value
                self.token = got
                continue
            self.token = block
            self.got[name] = self.swap(block, bit)

    def finish(self, names):
        while left := [name for name in names if name not in self.results]:
            self.advance(left)
        return [self.results[name] for name in names]


def per_device(
    cube,
    tokens,
    memory,
    token_segments,
    memory_segments,
    padding,
    self_project,
    self_output,
    cross_project,
    cross_output,
    widen_weight,
    narrow_weight,
    norm_gain,
    norm_bias,
    grad_out,
):
    token_low = tokens[0]
    memory_low = memory[0]
    row_in = token_low.astype(jnp.float32)
    segment_row = token_segments[0]
    places = jnp.arange(segment_row.shape[0])
    diagonal = places[None, :] == places[:, None]
    live_keys = padding[0] == 1
    self_allowed = (
        (segment_row[:, None] == segment_row[None, :])
        & (places[None, :] <= places[:, None])
        & (live_keys[None, :] | diagonal)
    )
    cross_allowed = segment_row[:, None] == memory_segments[0][None, :]
    pad_scale = padding[0].astype(jnp.float32)[:, None]
    width = token_low.shape[1]
    own = self_project.shape[1]
    hidden_width = widen_weight.shape[1]
    count, far = cube.count, cube.far
    orders = cube.orders
    side = lax.axis_index("pair")
    drive = Driver(cube, GATHER_DEPTH)

    def both_sides(mine, other):
        return [jnp.where(side == 0, mine, other), jnp.where(side == 0, other, mine)]

    shard = widen_weight.reshape(own, far, 2, hidden_width // (2 * far))
    mine, other = (
        lax.dynamic_index_in_dim(shard, k, axis=2, keepdims=False).reshape(own, hidden_width // 2)
        for k in (side, 1 - side)
    )
    narrow_shard = jnp.concatenate([narrow_weight[: 2 * own], narrow_weight[2 * own :]], axis=1)
    wide_shard = jnp.concatenate(
        [*both_sides(mine, drive.swap(other, PAIR)), narrow_shard], axis=0
    ).reshape(4, own, 2 * width)

    def gather_wide():
        return lax.all_gather(drive.after(wide_shard), ("far", "core", "fsdp"), axis=1, tiled=True)

    def gather_cross():
        return lax.all_gather(drive.after(cross_project[1:]), AXES, axis=1, tiled=True)

    norm_rows = jnp.concatenate([norm_gain, norm_bias], axis=0)
    norm_rows = jnp.pad(norm_rows, ((0, 16 - 6), (0, width - own)))
    shared = orders["A"][:2:-1]
    self_shard = jnp.concatenate([self_project.reshape(3 * own, width), self_output, norm_rows], axis=0)
    cross_shard = jnp.concatenate([cross_project[0], cross_output], axis=0)
    drive.calls = {"wide": gather_wide, "cross": gather_cross}
    drive.starts = {
        "s": lambda: cube.spread(self_shard[None], shared),
        "c": lambda: cube.spread(cross_shard[None], shared),
        "s1": lambda: cube.gather(drive.finish(["s"])[0][:, : 2 * own], orders[GATHER["s1"]]),
        "s2": lambda: cube.gather(drive.finish(["s"])[0][:, 2 * own :], orders[GATHER["s2"]]),
        "c1": lambda: cube.gather(drive.finish(["c"])[0][:, :own], orders[GATHER["c1"]]),
        "c2": lambda: cube.gather(drive.finish(["c"])[0][:, own:], orders[GATHER["c2"]]),
    }
    drive.advance(STEPS["early"])
    drive.finish(["s", "c"])
    drive.advance(STEPS["self"])
    drive.finish(["s1", "s2"])
    query_full, key_full = cube.natural(drive.results["s1"], orders[GATHER["s1"]], [own, own], cube.place)
    value_full, self_final, norms = cube.natural(drive.results["s2"], orders[GATHER["s2"]], [own, own, 16], cube.place)
    self_stack = [query_full, key_full, value_full]
    norms = norms.reshape(count, 16, width)[:, :6, :own].transpose(1, 0, 2).reshape(6, width)
    norms = norms.astype(jnp.float32)
    gain_values, bias_values = norms[:3], norms[3:]

    self_query, self_key, self_value = project_three(token_low, token_low, self_stack)
    self_mixed, self_logsum = attend_forward(self_query, self_key, self_value, self_allowed)
    pre_one = ALPHA * row_in + product(self_mixed, self_final)
    first_out = normalize(pre_one, gain_values[0], bias_values[0])
    first_low = rounded(first_out)

    drive.done(first_low)
    drive.advance(STEPS["cross"])
    drive.finish(["c1", "c2"])
    drive.finish(["wide", "cross"])
    (query_full,) = cube.natural(drive.results["c1"], orders[GATHER["c1"]], [own], cube.place)
    (cross_final,) = cube.natural(drive.results["c2"], orders[GATHER["c2"]], [own], cube.place)
    cross_stack = [query_full, *drive.results["cross"]]
    cross_query, cross_key, cross_value = project_three(first_low, memory_low, cross_stack)
    cross_mixed, cross_logsum = attend_forward(cross_query, cross_key, cross_value, cross_allowed)
    pre_two = ALPHA * first_out + product(cross_mixed, cross_final)
    second = normalize(pre_two, gain_values[1], bias_values[1])
    second_low = rounded(second)

    widen_full, narrow_full = cube.unpacked(drive.results["wide"])

    def widened(rows_low):
        hidden = product(rows_low, widen_full)
        active = rounded(jax.nn.gelu(hidden))
        return hidden, active, product(active, narrow_full)

    second_other = cube.swap(second_low, PAIR)
    hidden, active, branch = widened(second_low)
    hidden_other, active_other, branch_other = widened(second_other)
    branch_got = cube.swap(rounded(branch_other), PAIR)
    pre_three = ALPHA * second + (branch + branch_got.astype(jnp.float32))
    third_out = normalize(pre_three, gain_values[2], bias_values[2])
    layer_out = rounded(third_out * pad_scale)

    (self_mixed_turned,) = cube.turned([self_mixed], [orders[SCATTER["S2"]]], cube.place)
    token_turned = cube.turned([token_low], [orders[SCATTER["S1"]], orders[SCATTER["S2"]]], cube.place)
    (first_turned,) = cube.turned([first_low], [orders[SCATTER["P2"]]], cube.place)
    (memory_turned,) = cube.turned([memory_low], [orders[SCATTER["P1"]]], cube.place)
    (cross_mixed_turned,) = cube.turned([cross_mixed], [orders[SCATTER["P2"]]], cube.place)
    (second_turned,) = cube.turned([second_low, second_other], [[*orders[SCATTER["W"]], PAIR]], cube.place)
    (active_turned,) = cube.turned([active, active_other], [orders[SCATTER["N"]]], cube.side_place)
    drive = Driver(cube, SCATTER_DEPTH)

    grad_third = grad_out[0].astype(jnp.float32) * pad_scale
    grad_pre_three, grad_gain_three, grad_bias_three = normalize_back(
        pre_three, gain_values[2], bias_values[2], grad_third
    )
    ffn_branch = rounded(grad_pre_three)

    def widened_back(branch_low, hidden):
        grad_active = product(branch_low, narrow_full.T)
        unused, gelu_pull = jax.vjp(jax.nn.gelu, hidden)
        grad_hidden = rounded(gelu_pull(grad_active)[0])
        return grad_hidden, product(grad_hidden, widen_full.T)

    ffn_branch_other = cube.swap(ffn_branch, PAIR)
    grad_hidden, grad_branch = widened_back(ffn_branch, hidden)
    grad_hidden_other, grad_branch_other = widened_back(ffn_branch_other, hidden_other)
    grad_branch_got = drive.swap(drive.done(rounded(grad_branch_other)), PAIR)
    drive.add(
        "N",
        cube.scatter(
            [(drive.after(active_turned), jnp.concatenate([ffn_branch, ffn_branch_other], axis=0))], orders[SCATTER["N"]]
        ),
    )
    drive.add(
        "W",
        cube.scatter_pair(
            [(drive.after(second_turned), jnp.concatenate([grad_hidden, grad_hidden_other], axis=0))],
            orders[SCATTER["W"]],
        ),
    )
    grad_branch_got = drive.after(grad_branch_got)
    grad_second = ALPHA * grad_pre_three + (grad_branch + grad_branch_got.astype(jnp.float32))

    grad_pre_two, grad_gain_two, grad_bias_two = normalize_back(
        pre_two, gain_values[1], bias_values[1], grad_second
    )
    cross_branch = drive.done(rounded(grad_pre_two))
    drive.advance(STEPS["gs"])
    cross_branch = drive.after(cross_branch)
    grad_mixed = rounded(product(cross_branch, cross_final.T))
    cross_dq, cross_dk, cross_dv = attend_backward(
        cross_query, cross_key, cross_value, cross_allowed, cross_logsum, grad_mixed
    )
    grad_first_in, grad_memory = project_inputs(cross_stack, cross_dq, cross_dk, cross_dv)
    grad_first = ALPHA * grad_pre_two + grad_first_in
    drive.add(
        "P1",
        cube.scatter([(memory_turned, jnp.concatenate([cross_dk, cross_dv], axis=1))], orders[SCATTER["P1"]]),
    )
    drive.add(
        "P2",
        cube.scatter([(first_turned, cross_dq), (cross_mixed_turned, cross_branch)], orders[SCATTER["P2"]]),
    )
    drive.advance(STEPS["gf"])
    grad_first = drive.after(grad_first)

    grad_pre_one, grad_gain_one, grad_bias_one = normalize_back(
        pre_one, gain_values[0], bias_values[0], grad_first
    )
    self_branch = rounded(grad_pre_one)
    grad_mixed = rounded(product(self_branch, self_final.T))
    self_dq, self_dk, self_dv = attend_backward(
        self_query, self_key, self_value, self_allowed, self_logsum, grad_mixed
    )
    grad_query_in, grad_key_in = project_inputs(self_stack, self_dq, self_dk, self_dv)
    grad_tokens = ALPHA * grad_pre_one + grad_query_in + grad_key_in
    grad_norms = lax.optimization_barrier(
        jnp.stack(
            [
                grad_gain_one,
                grad_gain_two,
                grad_gain_three,
                grad_bias_one,
                grad_bias_two,
                grad_bias_three,
            ]
        )
    )
    drive.advance(STEPS["pre"])
    drive.add(
        "S1",
        cube.scatter(
            [(drive.after(token_turned[0]), jnp.concatenate([self_dq, self_dk], axis=1))], orders[SCATTER["S1"]]
        ),
    )
    drive.add(
        "S2",
        cube.scatter(
            [(drive.after(token_turned[1]), self_dv), (self_mixed_turned, self_branch)],
            orders[SCATTER["S2"]],
            cube.columns(grad_norms, orders[SCATTER["S2"]]),
        ),
    )
    drive.advance(STEPS["tail"])
    drive.finish(["N", "W", "P1", "P2", "S1", "S2"])
    sums = drive.results
    grad_norms = sums["S2"][:, 2 * width : 2 * width + 6].T
    widen_mine, widen_other = sums["W"]
    grad_widen = jnp.stack(
        [
            block.reshape(own, far, hidden_width // (2 * far))
            for block in both_sides(widen_mine, widen_other)
        ],
        axis=2,
    ).reshape(own, hidden_width)
    return (
        layer_out[None],
        grad_tokens[None],
        grad_memory[None],
        jnp.stack([sums["S1"][:, :width], sums["S1"][:, width:], sums["S2"][:, :width]]),
        sums["S2"][:, width : 2 * width],
        jnp.stack([sums["P2"][:, :width], sums["P1"][:, :width], sums["P1"][:, width:]]),
        sums["P2"][:, width:],
        grad_widen,
        sums["N"],
        grad_norms[:3],
        grad_norms[3:],
    )


def solution(mesh):
    cube = Cube(mesh)
    return jax.shard_map(
        functools.partial(per_device, cube),
        mesh=cube.mesh,
        in_specs=(
            P(AXES, None, None),
            P(AXES, None, None),
            P(AXES, None),
            P(AXES, None),
            P(AXES, None),
            P(None, AXES, None),
            P(AXES, None),
            P(None, AXES, None),
            P(AXES, None),
            P(AXES, None),
            P(AXES, None),
            P(None, AXES),
            P(None, AXES),
            P(AXES, None, None),
        ),
        out_specs=(
            P(AXES, None, None),
            P(AXES, None, None),
            P(AXES, None, None),
            P(None, AXES, None),
            P(AXES, None),
            P(None, AXES, None),
            P(AXES, None),
            P(AXES, None),
            P(AXES, None),
            P(None, AXES),
            P(None, AXES),
        ),
        check_vma=False,
    )
```

```python
import functools

import jax
import jax.numpy as jnp
import numpy as np
from jax import lax
from jax.experimental import pallas as pl
from jax.experimental.pallas import tpu as pltpu
from jax.sharding import PartitionSpec as P

HEADS = 16
HEAD = 64


ALPHA = (3.0 * 200.0) ** 0.25
EPSILON = 1e-05
MASKED = -1e30


def rounded(values_in):
    return values_in.astype(jnp.bfloat16)


def product(first_side, other_side):
    return jnp.dot(first_side, other_side, preferred_element_type=jnp.float32)


AXES = ("far", "pair", "core", "fsdp")
PAIR = ("pair", 0)
CORE = ("core", 0)
GATHER_DEPTH = 2
SCATTER_DEPTH = 4
GATHER = {"s1": "A", "s2": "B", "c1": "A", "c2": "B"}
SCATTER = {"N": "E", "W": "F", "P1": "B", "P2": "D", "S1": "A", "S2": "B"}
STEPS = {
    "gs": ["W", "N"],
    "gf": ["P2", "P1", "W", "N"],
    "pre": ["P2", "P1"],
    "tail": ["S1", "S2", "W", "N", "P2", "P1", "norms", "S1", "S2", "norms", "W", "N", "P2", "P1", "norms", "S2", "S1", "W", "norms", "P2", "P1", "norms", "S2", "S1", "norms", "S2", "S1"],
    "early": ["s", "cross", "s", "c", "s", "s1", "s2", "c"],
    "self": ["s1", "s2", "c", "wide", "c1", "c2", "s1", "s2", "c1", "c2", "s1", "s2"],
    "cross": ["c1", "c2", "c1", "c2"],
    "mid": [],
}


def normalize(values_in, scale_row, shift_row):
    average = jnp.mean(values_in, axis=-1, keepdims=True)
    centred = values_in - average
    spread = jnp.mean(centred * centred, axis=-1, keepdims=True)
    return centred * lax.rsqrt(spread + EPSILON) * scale_row + shift_row


def normalize_back(values_in, scale_row, shift_row, grad_result):
    unused, pullback = jax.vjp(normalize, values_in, scale_row, shift_row)
    return pullback(grad_result)


def project_three(query_source, key_source, weight_stack):
    return (
        rounded(product(query_source, weight_stack[0])),
        rounded(product(key_source, weight_stack[1])),
        rounded(product(key_source, weight_stack[2])),
    )


def project_inputs(weight_stack, grad_query, grad_key, grad_value):
    grad_query_side = product(grad_query, weight_stack[0].T)
    grad_key_side = product(grad_key, weight_stack[1].T) + product(grad_value, weight_stack[2].T)
    return (grad_query_side, grad_key_side)


def attend_forward(queries, key_rows, values, allowed):
    length, width = queries.shape
    lanes = 2 * HEAD

    def body(q_ref, k_ref, v_ref, allowed_ref, mixed_ref, logsum_ref):
        kept = allowed_ref[...] > 0.0
        lane = lax.broadcasted_iota(jnp.int32, (1, lanes), 1)
        for pair in range(width // lanes):
            columns = pl.ds(pair * lanes, lanes)
            query, key_block, value = (ref[:, columns] for ref in (q_ref, k_ref, v_ref))
            mixed = 0.0
            for half in range(2):
                head = 2 * pair + half
                here = ((lane // HEAD) == half).astype(jnp.float32).astype(jnp.bfloat16)
                scores = across(query * here, key_block, 1, 1) * HEAD ** (-0.5)
                scores = jnp.where(kept, scores, MASKED)
                largest = jnp.max(scores, axis=-1, keepdims=True)
                exponentials = jnp.exp(scores - largest)
                totals = jnp.sum(exponentials, axis=-1, keepdims=True)
                mixed += across(rounded(exponentials / totals), value * here, 1, 0)
                logsum_ref[:, head : head + 1] = largest + jnp.log(totals)
            mixed_ref[:, columns] = rounded(mixed)

    vmem = pl.BlockSpec(memory_space=pltpu.VMEM)
    return pl.pallas_call(
        body,
        out_shape=[
            jax.ShapeDtypeStruct((length, width), queries.dtype),
            jax.ShapeDtypeStruct((length, width // HEAD), jnp.float32),
        ],
        in_specs=[vmem] * 4,
        out_specs=[vmem] * 2,
        compiler_params=pltpu.CompilerParams(vmem_limit_bytes=40 * 2**20),
        cost_estimate=pl.CostEstimate(flops=1, bytes_accessed=1, transcendentals=0),
        name="attend_forward",
    )(queries, key_rows, values, allowed.astype(jnp.float32))


def attend_backward(queries, key_rows, values, allowed, logsum, grad_mixed, groups):
    length, width = queries.shape
    key_count, lanes = key_rows.shape[0], 2 * HEAD
    heights = {"q": length, "k": key_count, "v": key_count}

    def body(q_ref, k_ref, v_ref, grad_ref, allowed_ref, logsum_ref, *outs):
        kept = allowed_ref[...] > 0.0
        lane = lax.broadcasted_iota(jnp.int32, (1, lanes), 1)
        for pair in range(width // lanes):
            columns = pl.ds(pair * lanes, lanes)
            query, key_block, value, grad = (
                ref[:, columns] for ref in (q_ref, k_ref, v_ref, grad_ref)
            )
            totals = {"q": 0.0, "k": 0.0, "v": 0.0}
            for half in range(2):
                head = 2 * pair + half
                here = ((lane // HEAD) == half).astype(jnp.float32).astype(jnp.bfloat16)
                query_half, key_half, grad_half = query * here, key_block * here, grad * here
                scores = across(query_half, key_block, 1, 1) * HEAD ** (-0.5)
                weights = jnp.exp(jnp.where(kept, scores, MASKED) - logsum_ref[:, head : head + 1])
                grad_weights = across(grad_half, value, 1, 1)
                inner_sum = jnp.sum(weights * grad_weights, axis=-1, keepdims=True)
                grad_scores = rounded(weights * (grad_weights - inner_sum))
                totals["q"] += across(grad_scores, key_half, 1, 0)
                totals["k"] += across(grad_scores, query_half, 0, 0)
                totals["v"] += across(rounded(weights), grad_half, 0, 0)
            totals["q"] *= HEAD ** (-0.5)
            totals["k"] *= HEAD ** (-0.5)
            for group, out in zip(groups, outs):
                for k, name in enumerate(group):
                    out[:, pl.ds(k * width + pair * lanes, lanes)] = rounded(totals[name])

    vmem = pl.BlockSpec(memory_space=pltpu.VMEM)
    return pl.pallas_call(
        body,
        out_shape=[
            jax.ShapeDtypeStruct((heights[group[0]], len(group) * width), queries.dtype) for group in groups
        ],
        in_specs=[vmem] * 6,
        out_specs=[vmem for _ in groups],
        compiler_params=pltpu.CompilerParams(vmem_limit_bytes=40 * 2**20),
        cost_estimate=pl.CostEstimate(flops=1, bytes_accessed=1, transcendentals=0),
        name="attend_backward",
    )(
        queries,
        key_rows,
        values,
        grad_mixed,
        allowed.astype(jnp.float32),
        logsum,
    )


def across(one, other, one_dim, other_dim):
    return lax.dot_general(
        one, other, (((one_dim,), (other_dim,)), ((), ())), preferred_element_type=jnp.float32
    )


class Cube:
    def __init__(self, mesh):
        far, inner = mesh.shape["dp"] // 4, mesh.shape["fsdp"]
        self.mesh = jax.sharding.Mesh(mesh.devices.reshape(far, 2, 2, inner), AXES)
        self.sizes = dict(zip(AXES, (far, 2, 2, inner)))
        self.count = 4 * far * inner
        self.far = far
        close = [("fsdp", k) for k in range(inner.bit_length() - 1)]
        apart = [("far", k) for k in range(far.bit_length() - 1)]
        self.place = {bit: k for k, bit in enumerate([*close, CORE, PAIR, *apart])}
        self.side_place = {bit: k for k, bit in enumerate([*close, CORE, *apart])}
        self.orders = {
            "A": [CORE, close[0], PAIR, *close[1:], *apart],
            "B": [CORE, PAIR, *close, *apart],
            "C": [CORE, close[1], close[0], PAIR, *close[2:], *apart],
            "D": [CORE, close[1], PAIR, close[0], *close[2:], *apart],
            "E": [CORE, *close, *apart],
            "F": [CORE, close[1], close[0], *close[2:], *apart],
            "H": [CORE, *close[1:], close[0], *apart],
        }

    def index(self, place):
        return sum(((lax.axis_index(axis) >> k) & 1) << shift for (axis, k), shift in place.items())

    def swap(self, block, bit):
        axis, k = bit
        return lax.ppermute(block, axis, [(i, i ^ (1 << k)) for i in range(self.sizes[axis])])

    def offsets(self, order, place):
        last = len(order) - 1
        return [
            sum(1 << place[bit] for k, bit in enumerate(order) if (p >> (last - k)) & 1)
            for p in range(1 << len(order))
        ]

    def spread(self, held, bits):
        for bit in bits:
            held = jnp.concatenate([held, (yield held, bit)], axis=0)
        return held

    def gather(self, held, order):
        done = held.shape[0].bit_length() - 1
        held = yield from self.spread(held, order[:0:-1][done:])
        return held, (yield held, order[0])

    def natural(self, halves, order, segments, place):
        low, high = halves
        offsets = self.offsets(order, place)
        count, half = 2 * low.shape[0], low.shape[0]
        columns = low.shape[2]
        starts = [sum(segments[:k]) for k in range(len(segments))]
        index = self.index(place)
        if any(rows % 16 for rows in segments):
            where = np.argsort(np.array(offsets))
            picked = jnp.asarray(where)[jnp.arange(count) ^ index]
            blocks = jnp.take(jnp.concatenate(halves, axis=0), picked, axis=0)
            return [
                blocks[:, start : start + rows].reshape(count * rows, columns)
                for start, rows in zip(starts, segments)
            ]
        pieces = list(enumerate(zip(starts, segments)))

        def body(index_ref, low_ref, high_ref, *refs):
            index, sems = index_ref[0], refs[-1]
            copies = []
            for p in range(count):
                source = low_ref.at[p] if p < half else high_ref.at[p - half]
                for k, (start, rows) in pieces:
                    copies.append(
                        pltpu.make_async_copy(
                            source.at[pl.ds(start, rows)], refs[k].at[index ^ offsets[p]], sems.at[p, k]
                        )
                    )
                    copies[-1].start()
            for copy in copies:
                copy.wait()

        moved = pl.pallas_call(
            body,
            out_shape=[jax.ShapeDtypeStruct((count, rows, columns), low.dtype) for rows in segments],
            in_specs=[
                pl.BlockSpec(memory_space=pltpu.SMEM),
                pl.BlockSpec(memory_space=pl.ANY),
                pl.BlockSpec(memory_space=pl.ANY),
            ],
            out_specs=[pl.BlockSpec(memory_space=pltpu.VMEM) for _ in segments],
            scratch_shapes=[pltpu.SemaphoreType.DMA((count, len(segments)))],
            compiler_params=pltpu.CompilerParams(vmem_limit_bytes=40 * 2**20),
            name="natural_order",
        )(index.astype(jnp.int32).reshape(1), low, high)
        return [block.reshape(count * rows, columns) for block, rows in zip(moved, segments)]

    def unpacked(self, packed):
        rows, columns = packed.shape[1] // (self.count // 2), packed.shape[2]
        count, far, half = self.count // 2, self.far, columns // 2

        def widen(blocks):
            return blocks.reshape(2, far, -1, columns).transpose(1, 0, 2, 3).reshape(-1, columns)

        if rows % 16:
            narrow = packed[2:].reshape(2, count, rows, 2, half).transpose(1, 3, 0, 2, 4)
            return widen(packed[:2]), narrow.reshape(-1, half)

        def body(packed_ref, widen_ref, narrow_ref, sems):
            copies = [pltpu.make_async_copy(packed_ref.at[pl.ds(0, 2)], widen_ref, sems.at[0])]
            for p in range(count):
                for k in range(4):
                    source = packed_ref.at[
                        2 + k % 2, pl.ds(p * rows, rows), pl.ds((k // 2) * half, half)
                    ]
                    copies.append(
                        pltpu.make_async_copy(
                            source, narrow_ref.at[p, pl.ds(k * rows, rows)], sems.at[1 + 4 * p + k]
                        )
                    )
            for copy in copies:
                copy.start()
            for copy in copies:
                copy.wait()

        wide, narrow = pl.pallas_call(
            body,
            out_shape=[
                jax.ShapeDtypeStruct((2, count * rows, columns), packed.dtype),
                jax.ShapeDtypeStruct((count, 4 * rows, half), packed.dtype),
            ],
            in_specs=[pl.BlockSpec(memory_space=pl.ANY)],
            out_specs=[pl.BlockSpec(memory_space=pltpu.VMEM)] * 2,
            scratch_shapes=[pltpu.SemaphoreType.DMA((1 + 4 * count,))],
            compiler_params=pltpu.CompilerParams(vmem_limit_bytes=40 * 2**20),
            name="unpacked",
        )(packed)
        return widen(wide), narrow.reshape(-1, half)

    def turned(self, sources, orders, place):
        tokens, features = sources[0].shape
        count = 1 << len(place)
        rows, wide = features // count, tokens * len(sources)
        tables = [self.offsets(order, place) for order in orders]
        index = self.index(place)
        if rows % 16:
            blocks = jnp.concatenate(sources, axis=0).T.reshape(count, rows, wide)
            return [jnp.take(blocks, jnp.asarray(table) ^ index, axis=0) for table in tables]

        def body(index_ref, *refs):
            index = index_ref[0]
            ins, outs, held = refs[: len(sources)], refs[len(sources) : -1], refs[-1]
            for k, in_ref in enumerate(ins):
                held[:, :, pl.ds(k * tokens, tokens)] = in_ref[...].T.reshape(count, rows, tokens)
            for table, out in zip(tables, outs):
                for p in range(count):
                    out[p] = held[index ^ table[p]]

        shape = (count, rows, wide)
        return pl.pallas_call(
            body,
            out_shape=[jax.ShapeDtypeStruct(shape, sources[0].dtype) for _ in tables],
            in_specs=[pl.BlockSpec(memory_space=pltpu.SMEM)]
            + [pl.BlockSpec(memory_space=pltpu.VMEM) for _ in sources],
            out_specs=[pl.BlockSpec(memory_space=pltpu.VMEM) for _ in tables],
            scratch_shapes=[pltpu.VMEM(shape, sources[0].dtype)],
            compiler_params=pltpu.CompilerParams(vmem_limit_bytes=40 * 2**20),
            name="turned",
        )(index.astype(jnp.int32).reshape(1), *sources)

    def scatter(self, sides, order):
        blocks = 1 << len(order)
        half, quarter = blocks // 2, blocks // 4

        def parts(first, last, got=None):
            terms, column = [], 0
            for turned, other in sides:
                rows = turned.shape[0] // blocks
                block = turned[first * rows : last * rows]
                term = product(block.reshape(-1, turned.shape[-1]), other)
                if got is not None:
                    term = term + got[:, column : column + term.shape[1]].astype(jnp.float32)
                column += term.shape[1]
                terms.append(term)
            return terms

        def joined(terms):
            return terms[0] if len(terms) == 1 else jnp.concatenate(terms, axis=1)

        got = yield joined([rounded(term) for term in parts(half, blocks)]), order[0]
        middle = got.shape[0] // 2
        sent = joined([rounded(term) for term in parts(quarter, half, got[middle:])])
        kept = joined(parts(0, quarter, got[:middle]))
        for bit in order[1:-1]:
            got = yield sent, bit
            middle = kept.shape[0] // 2
            sent = rounded(kept[middle:] + got[middle:].astype(jnp.float32))
            kept = kept[:middle] + got[:middle].astype(jnp.float32)
        return kept + (yield sent, order[-1]).astype(jnp.float32)

    def scatter_pair(self, sides, order):
        kept = yield from self.scatter(sides, order)
        middle = kept.shape[0] // 2
        got = (yield rounded(kept[middle:]), PAIR).astype(jnp.float32)
        return kept[:middle], got

    def scatter_small(self, rows_in, order):
        lines, features = rows_in.shape
        own = features // self.count
        blocks = rows_in.reshape(lines, self.count, own).transpose(1, 0, 2)
        blocks = jnp.pad(blocks, ((0, 0), (0, 8 - lines), (0, 128 - own)))
        table = jnp.asarray(self.offsets(order, self.place))
        held = jnp.take(blocks, table ^ self.index(self.place), axis=0)
        for bit in order:
            middle = held.shape[0] // 2
            held = held[:middle] + (yield held[middle:], bit)
        return held[0, :lines, :own]


class Driver:
    def __init__(self, cube, depth):
        self.cube, self.depth = cube, depth
        self.before = {bit: [] for bit in cube.place}
        self.chains, self.got, self.results = {}, {}, {}
        self.token = None
        self.starts, self.calls = {}, {}

    def swap(self, block, bit):
        past = self.before[bit]
        if len(past) >= self.depth:
            block, _ = lax.optimization_barrier((block, past[-self.depth]))
        past.append(self.cube.swap(block, bit))
        return past[-1]

    def after(self, block):
        if self.token is None:
            return block
        return lax.optimization_barrier((block, self.token))[0]

    def done(self, block):
        self.token = block
        return block

    def add(self, name, chain):
        self.chains[name] = chain
        block, bit = next(chain)
        self.token = block
        self.got[name] = self.swap(block, bit)

    def advance(self, names):
        for name in names:
            if name in self.calls:
                self.results[name] = self.calls.pop(name)()
                continue
            if name in self.starts:
                self.add(name, self.starts.pop(name)())
                continue
            if name in self.results:
                continue
            got = self.after(self.got[name])
            try:
                block, bit = self.chains[name].send(got)
            except StopIteration as stop:
                self.results[name] = stop.value
                self.token = got
                continue
            self.token = block
            self.got[name] = self.swap(block, bit)

    def finish(self, names):
        while left := [name for name in names if name not in self.results]:
            self.advance(left)
        return [self.results[name] for name in names]


def per_device(
    cube,
    tokens,
    memory,
    token_segments,
    memory_segments,
    padding,
    self_project,
    self_output,
    cross_project,
    cross_output,
    widen_weight,
    narrow_weight,
    norm_gain,
    norm_bias,
    grad_out,
):
    token_low = tokens[0]
    memory_low = memory[0]
    row_in = token_low.astype(jnp.float32)
    segment_row = token_segments[0]
    places = jnp.arange(segment_row.shape[0])
    diagonal = places[None, :] == places[:, None]
    live_keys = padding[0] == 1
    self_allowed = (
        (segment_row[:, None] == segment_row[None, :])
        & (places[None, :] <= places[:, None])
        & (live_keys[None, :] | diagonal)
    )
    cross_allowed = segment_row[:, None] == memory_segments[0][None, :]
    pad_scale = padding[0].astype(jnp.float32)[:, None]
    width = token_low.shape[1]
    own = self_project.shape[1]
    hidden_width = widen_weight.shape[1]
    count, far = cube.count, cube.far
    orders = cube.orders
    side = lax.axis_index("pair")
    drive = Driver(cube, GATHER_DEPTH)

    def both_sides(mine, other):
        return [jnp.where(side == 0, mine, other), jnp.where(side == 0, other, mine)]

    shard = widen_weight.reshape(own, far, 2, hidden_width // (2 * far))
    mine, other = (
        lax.dynamic_index_in_dim(shard, k, axis=2, keepdims=False).reshape(own, hidden_width // 2)
        for k in (side, 1 - side)
    )
    narrow_shard = jnp.concatenate([narrow_weight[: 2 * own], narrow_weight[2 * own :]], axis=1)
    wide_shard = jnp.concatenate(
        [*both_sides(mine, drive.swap(other, PAIR)), narrow_shard], axis=0
    ).reshape(4, own, 2 * width)

    def gather_wide():
        return lax.all_gather(drive.after(wide_shard), ("far", "core", "fsdp"), axis=1, tiled=True)

    def gather_cross():
        return lax.all_gather(drive.after(cross_project[1:]), AXES, axis=1, tiled=True)

    norm_rows = jnp.concatenate([norm_gain, norm_bias], axis=0)
    norm_rows = jnp.pad(norm_rows, ((0, 16 - 6), (0, width - own)))
    shared = orders["A"][:2:-1]
    self_shard = jnp.concatenate([self_project.reshape(3 * own, width), self_output, norm_rows], axis=0)
    cross_shard = jnp.concatenate([cross_project[0], cross_output], axis=0)
    drive.calls = {"wide": gather_wide, "cross": gather_cross}
    drive.starts = {
        "s": lambda: cube.spread(self_shard[None], shared),
        "c": lambda: cube.spread(cross_shard[None], shared),
        "s1": lambda: cube.gather(drive.finish(["s"])[0][:, : 2 * own], orders[GATHER["s1"]]),
        "s2": lambda: cube.gather(drive.finish(["s"])[0][:, 2 * own :], orders[GATHER["s2"]]),
        "c1": lambda: cube.gather(drive.finish(["c"])[0][:, :own], orders[GATHER["c1"]]),
        "c2": lambda: cube.gather(drive.finish(["c"])[0][:, own:], orders[GATHER["c2"]]),
    }
    drive.advance(STEPS["early"])
    drive.finish(["s", "c"])
    drive.advance(STEPS["self"])
    drive.finish(["s1", "s2"])
    query_full, key_full = cube.natural(drive.results["s1"], orders[GATHER["s1"]], [own, own], cube.place)
    value_full, self_final, norms = cube.natural(drive.results["s2"], orders[GATHER["s2"]], [own, own, 16], cube.place)
    self_stack = [query_full, key_full, value_full]
    norms = norms.reshape(count, 16, width)[:, :6, :own].transpose(1, 0, 2).reshape(6, width)
    norms = norms.astype(jnp.float32)
    gain_values, bias_values = norms[:3], norms[3:]

    self_query, self_key, self_value = project_three(token_low, token_low, self_stack)
    self_mixed, self_logsum = attend_forward(self_query, self_key, self_value, self_allowed)
    pre_one = ALPHA * row_in + product(self_mixed, self_final)
    first_out = normalize(pre_one, gain_values[0], bias_values[0])
    first_low = rounded(first_out)

    drive.done(first_low)
    drive.advance(STEPS["cross"])
    drive.finish(["c1", "c2"])
    drive.finish(["wide", "cross"])
    (query_full,) = cube.natural(drive.results["c1"], orders[GATHER["c1"]], [own], cube.place)
    (cross_final,) = cube.natural(drive.results["c2"], orders[GATHER["c2"]], [own], cube.place)
    cross_stack = [query_full, *drive.results["cross"]]
    cross_query, cross_key, cross_value = project_three(first_low, memory_low, cross_stack)
    cross_mixed, cross_logsum = attend_forward(cross_query, cross_key, cross_value, cross_allowed)
    pre_two = ALPHA * first_out + product(cross_mixed, cross_final)
    second = normalize(pre_two, gain_values[1], bias_values[1])
    second_low = rounded(second)

    widen_full, narrow_full = cube.unpacked(drive.results["wide"])

    def widened(rows_low):
        hidden = product(rows_low, widen_full)
        active = rounded(jax.nn.gelu(hidden))
        return hidden, active, product(active, narrow_full)

    second_other = cube.swap(second_low, PAIR)
    hidden, active, branch = widened(second_low)
    hidden_other, active_other, branch_other = widened(second_other)
    branch_got = cube.swap(rounded(branch_other), PAIR)
    pre_three = ALPHA * second + (branch + branch_got.astype(jnp.float32))
    third_out = normalize(pre_three, gain_values[2], bias_values[2])
    layer_out = rounded(third_out * pad_scale)

    (self_mixed_turned,) = cube.turned([self_mixed], [orders[SCATTER["S2"]]], cube.place)
    token_turned = cube.turned([token_low], [orders[SCATTER["S1"]], orders[SCATTER["S2"]]], cube.place)
    (first_turned,) = cube.turned([first_low], [orders[SCATTER["P2"]]], cube.place)
    (memory_turned,) = cube.turned([memory_low], [orders[SCATTER["P1"]]], cube.place)
    (cross_mixed_turned,) = cube.turned([cross_mixed], [orders[SCATTER["P2"]]], cube.place)
    (second_turned,) = cube.turned([second_low, second_other], [[*orders[SCATTER["W"]], PAIR]], cube.place)
    (active_turned,) = cube.turned([active, active_other], [orders[SCATTER["N"]]], cube.side_place)
    drive = Driver(cube, SCATTER_DEPTH)

    grad_third = grad_out[0].astype(jnp.float32) * pad_scale
    grad_pre_three, grad_gain_three, grad_bias_three = normalize_back(
        pre_three, gain_values[2], bias_values[2], grad_third
    )
    ffn_branch = rounded(grad_pre_three)

    def widened_back(branch_low, hidden):
        grad_active = product(branch_low, narrow_full.T)
        unused, gelu_pull = jax.vjp(jax.nn.gelu, hidden)
        grad_hidden = rounded(gelu_pull(grad_active)[0])
        return grad_hidden, product(grad_hidden, widen_full.T)

    ffn_branch_other = cube.swap(ffn_branch, PAIR)
    grad_hidden, grad_branch = widened_back(ffn_branch, hidden)
    grad_hidden_other, grad_branch_other = widened_back(ffn_branch_other, hidden_other)
    grad_branch_got = drive.swap(drive.done(rounded(grad_branch_other)), PAIR)
    drive.add(
        "N",
        cube.scatter(
            [(drive.after(active_turned), jnp.concatenate([ffn_branch, ffn_branch_other], axis=0))], orders[SCATTER["N"]]
        ),
    )
    drive.add(
        "W",
        cube.scatter_pair(
            [(drive.after(second_turned), jnp.concatenate([grad_hidden, grad_hidden_other], axis=0))],
            orders[SCATTER["W"]],
        ),
    )
    grad_branch_got = drive.after(grad_branch_got)
    grad_second = ALPHA * grad_pre_three + (grad_branch + grad_branch_got.astype(jnp.float32))

    grad_pre_two, grad_gain_two, grad_bias_two = normalize_back(
        pre_two, gain_values[1], bias_values[1], grad_second
    )
    cross_branch = drive.done(rounded(grad_pre_two))
    drive.advance(STEPS["gs"])
    cross_branch = drive.after(cross_branch)
    grad_mixed = rounded(product(cross_branch, cross_final.T))
    cross_keys, cross_dq = attend_backward(
        cross_query, cross_key, cross_value, cross_allowed, cross_logsum, grad_mixed, (("k", "v"), ("q",))
    )
    cross_dk, cross_dv = cross_keys[:, :width], cross_keys[:, width:]
    grad_first = ALPHA * grad_pre_two + product(cross_dq, cross_stack[0].T)
    drive.add(
        "P1",
        cube.scatter([(memory_turned, cross_keys)], orders[SCATTER["P1"]]),
    )
    drive.add(
        "P2",
        cube.scatter([(first_turned, cross_dq), (cross_mixed_turned, cross_branch)], orders[SCATTER["P2"]]),
    )
    drive.advance(STEPS["gf"])
    grad_first = drive.after(grad_first)

    grad_pre_one, grad_gain_one, grad_bias_one = normalize_back(
        pre_one, gain_values[0], bias_values[0], grad_first
    )
    self_branch = rounded(grad_pre_one)
    grad_mixed = rounded(product(self_branch, self_final.T))
    self_keys, self_dv = attend_backward(
        self_query, self_key, self_value, self_allowed, self_logsum, grad_mixed, (("q", "k"), ("v",))
    )
    self_dq, self_dk = self_keys[:, :width], self_keys[:, width:]
    drive.advance(STEPS["pre"])
    drive.add(
        "S1",
        cube.scatter(
            [(drive.after(token_turned[0]), self_keys)], orders[SCATTER["S1"]]
        ),
    )
    drive.add(
        "S2",
        cube.scatter(
            [(drive.after(token_turned[1]), self_dv), (self_mixed_turned, self_branch)],
            orders[SCATTER["S2"]],
        ),
    )
    unused, grad_memory = project_inputs(cross_stack, cross_dq, drive.after(cross_dk), cross_dv)
    grad_query_in, grad_key_in = project_inputs(self_stack, drive.after(self_dq), self_dk, self_dv)
    grad_tokens = ALPHA * grad_pre_one + grad_query_in + grad_key_in
    norm_rows = lax.optimization_barrier(
        jnp.stack(
            [
                grad_gain_one,
                grad_gain_two,
                grad_gain_three,
                grad_bias_one,
                grad_bias_two,
                grad_bias_three,
            ]
        )
    )
    drive.starts = {"norms": lambda: cube.scatter_small(norm_rows, orders["B"])}
    drive.advance(STEPS["tail"])
    drive.finish(["norms", "N", "W", "P1", "P2", "S1", "S2"])
    sums = drive.results
    widen_mine, widen_other = sums["W"]
    grad_widen = jnp.stack(
        [
            block.reshape(own, far, hidden_width // (2 * far))
            for block in both_sides(widen_mine, widen_other)
        ],
        axis=2,
    ).reshape(own, hidden_width)
    return (
        layer_out[None],
        grad_tokens[None],
        grad_memory[None],
        jnp.stack([sums["S1"][:, :width], sums["S1"][:, width:], sums["S2"][:, :width]]),
        sums["S2"][:, width : 2 * width],
        jnp.stack([sums["P2"][:, :width], sums["P1"][:, :width], sums["P1"][:, width:]]),
        sums["P2"][:, width:],
        grad_widen,
        sums["N"],
        sums["norms"][:3],
        sums["norms"][3:],
    )


def solution(mesh):
    cube = Cube(mesh)
    return jax.shard_map(
        functools.partial(per_device, cube),
        mesh=cube.mesh,
        in_specs=(
            P(AXES, None, None),
            P(AXES, None, None),
            P(AXES, None),
            P(AXES, None),
            P(AXES, None),
            P(None, AXES, None),
            P(AXES, None),
            P(None, AXES, None),
            P(AXES, None),
            P(AXES, None),
            P(AXES, None),
            P(None, AXES),
            P(None, AXES),
            P(AXES, None, None),
        ),
        out_specs=(
            P(AXES, None, None),
            P(AXES, None, None),
            P(AXES, None, None),
            P(None, AXES, None),
            P(AXES, None),
            P(None, AXES, None),
            P(AXES, None),
            P(AXES, None),
            P(AXES, None),
            P(None, AXES),
            P(None, AXES),
        ),
        check_vma=False,
    )
```

```python
import functools

import jax
import jax.numpy as jnp
import numpy as np
from jax import lax
from jax.experimental import pallas as pl
from jax.experimental.pallas import tpu as pltpu
from jax.sharding import PartitionSpec as P

HEADS = 16
HEAD = 64


ALPHA = (3.0 * 200.0) ** 0.25
EPSILON = 1e-05
MASKED = -1e30


def rounded(values_in):
    return values_in.astype(jnp.bfloat16)


def product(first_side, other_side):
    return jnp.dot(first_side, other_side, preferred_element_type=jnp.float32)


AXES = ("far", "pair", "core", "fsdp")
PAIR = ("pair", 0)
CORE = ("core", 0)
GATHER_DEPTH = 2
SCATTER_DEPTH = 4
GATHER = {"s1": "A", "s2": "B", "c1": "A", "c2": "B"}
SCATTER = {"N": "E", "W": "F", "P1": "B", "P2": "D", "S1": "A", "S2": "B"}
STEPS = {
    "gs": ["W", "N"],
    "gf": ["P2", "P1", "W", "N"],
    "pre": ["P2", "P1"],
    "tail": ["S1", "S2", "W", "N", "P2", "P1", "S1", "S2", "W", "N", "P2", "P1", "S2", "S1", "W", "P2", "P1", "S2", "S1", "S2", "S1"],
    "early": ["s", "cross", "s", "c", "s", "s1", "s2", "c"],
    "self": ["s1", "s2", "c", "wide", "c1", "c2", "s1", "s2", "c1", "c2", "s1", "s2"],
    "cross": ["c1", "c2", "c1", "c2"],
    "mid": [],
}


def normalize(values_in, scale_row, shift_row):
    average = jnp.mean(values_in, axis=-1, keepdims=True)
    centred = values_in - average
    spread = jnp.mean(centred * centred, axis=-1, keepdims=True)
    return centred * lax.rsqrt(spread + EPSILON) * scale_row + shift_row


def normalize_back(values_in, scale_row, shift_row, grad_result):
    unused, pullback = jax.vjp(normalize, values_in, scale_row, shift_row)
    return pullback(grad_result)


def project_three(query_source, key_source, weight_stack):
    return (
        rounded(product(query_source, weight_stack[0])),
        rounded(product(key_source, weight_stack[1])),
        rounded(product(key_source, weight_stack[2])),
    )


def project_inputs(weight_stack, grad_query, grad_key, grad_value):
    grad_query_side = product(grad_query, weight_stack[0].T)
    grad_key_side = product(grad_key, weight_stack[1].T) + product(grad_value, weight_stack[2].T)
    return (grad_query_side, grad_key_side)


def attend_forward(queries, key_rows, values, allowed):
    length, width = queries.shape
    lanes = 2 * HEAD

    def body(q_ref, k_ref, v_ref, allowed_ref, mixed_ref, logsum_ref):
        kept = allowed_ref[...] > 0.0
        lane = lax.broadcasted_iota(jnp.int32, (1, lanes), 1)
        for pair in range(width // lanes):
            columns = pl.ds(pair * lanes, lanes)
            query, key_block, value = (ref[:, columns] for ref in (q_ref, k_ref, v_ref))
            mixed = 0.0
            for half in range(2):
                head = 2 * pair + half
                here = ((lane // HEAD) == half).astype(jnp.float32).astype(jnp.bfloat16)
                scores = across(query * here, key_block, 1, 1) * HEAD ** (-0.5)
                scores = jnp.where(kept, scores, MASKED)
                largest = jnp.max(scores, axis=-1, keepdims=True)
                exponentials = jnp.exp(scores - largest)
                totals = jnp.sum(exponentials, axis=-1, keepdims=True)
                mixed += across(rounded(exponentials / totals), value * here, 1, 0)
                logsum_ref[:, head : head + 1] = largest + jnp.log(totals)
            mixed_ref[:, columns] = rounded(mixed)

    vmem = pl.BlockSpec(memory_space=pltpu.VMEM)
    return pl.pallas_call(
        body,
        out_shape=[
            jax.ShapeDtypeStruct((length, width), queries.dtype),
            jax.ShapeDtypeStruct((length, width // HEAD), jnp.float32),
        ],
        in_specs=[vmem] * 4,
        out_specs=[vmem] * 2,
        compiler_params=pltpu.CompilerParams(vmem_limit_bytes=40 * 2**20),
        cost_estimate=pl.CostEstimate(flops=1, bytes_accessed=1, transcendentals=0),
        name="attend_forward",
    )(queries, key_rows, values, allowed.astype(jnp.float32))


def attend_backward(queries, key_rows, values, allowed, logsum, grad_mixed, groups):
    length, width = queries.shape
    key_count, lanes = key_rows.shape[0], 2 * HEAD
    heights = {"q": length, "k": key_count, "v": key_count}

    def body(q_ref, k_ref, v_ref, grad_ref, allowed_ref, logsum_ref, *outs):
        kept = allowed_ref[...] > 0.0
        lane = lax.broadcasted_iota(jnp.int32, (1, lanes), 1)
        for pair in range(width // lanes):
            columns = pl.ds(pair * lanes, lanes)
            query, key_block, value, grad = (
                ref[:, columns] for ref in (q_ref, k_ref, v_ref, grad_ref)
            )
            totals = {"q": 0.0, "k": 0.0, "v": 0.0}
            for half in range(2):
                head = 2 * pair + half
                here = ((lane // HEAD) == half).astype(jnp.float32).astype(jnp.bfloat16)
                query_half, key_half, grad_half = query * here, key_block * here, grad * here
                scores = across(query_half, key_block, 1, 1) * HEAD ** (-0.5)
                weights = jnp.exp(jnp.where(kept, scores, MASKED) - logsum_ref[:, head : head + 1])
                grad_weights = across(grad_half, value, 1, 1)
                inner_sum = jnp.sum(weights * grad_weights, axis=-1, keepdims=True)
                grad_scores = rounded(weights * (grad_weights - inner_sum))
                totals["q"] += across(grad_scores, key_half, 1, 0)
                totals["k"] += across(grad_scores, query_half, 0, 0)
                totals["v"] += across(rounded(weights), grad_half, 0, 0)
            totals["q"] *= HEAD ** (-0.5)
            totals["k"] *= HEAD ** (-0.5)
            for group, out in zip(groups, outs):
                for k, name in enumerate(group):
                    out[:, pl.ds(k * width + pair * lanes, lanes)] = rounded(totals[name])

    vmem = pl.BlockSpec(memory_space=pltpu.VMEM)
    return pl.pallas_call(
        body,
        out_shape=[
            jax.ShapeDtypeStruct((heights[group[0]], len(group) * width), queries.dtype) for group in groups
        ],
        in_specs=[vmem] * 6,
        out_specs=[vmem for _ in groups],
        compiler_params=pltpu.CompilerParams(vmem_limit_bytes=40 * 2**20),
        cost_estimate=pl.CostEstimate(flops=1, bytes_accessed=1, transcendentals=0),
        name="attend_backward",
    )(
        queries,
        key_rows,
        values,
        grad_mixed,
        allowed.astype(jnp.float32),
        logsum,
    )


def across(one, other, one_dim, other_dim):
    return lax.dot_general(
        one, other, (((one_dim,), (other_dim,)), ((), ())), preferred_element_type=jnp.float32
    )


class Cube:
    def __init__(self, mesh):
        far, inner = mesh.shape["dp"] // 4, mesh.shape["fsdp"]
        self.mesh = jax.sharding.Mesh(mesh.devices.reshape(far, 2, 2, inner), AXES)
        self.sizes = dict(zip(AXES, (far, 2, 2, inner)))
        self.count = 4 * far * inner
        self.far = far
        close = [("fsdp", k) for k in range(inner.bit_length() - 1)]
        apart = [("far", k) for k in range(far.bit_length() - 1)]
        self.place = {bit: k for k, bit in enumerate([*close, CORE, PAIR, *apart])}
        self.side_place = {bit: k for k, bit in enumerate([*close, CORE, *apart])}
        self.orders = {
            "A": [CORE, close[0], PAIR, *close[1:], *apart],
            "B": [CORE, PAIR, *close, *apart],
            "C": [CORE, close[1], close[0], PAIR, *close[2:], *apart],
            "D": [CORE, close[1], PAIR, close[0], *close[2:], *apart],
            "E": [CORE, *close, *apart],
            "F": [CORE, close[1], close[0], *close[2:], *apart],
            "H": [CORE, *close[1:], close[0], *apart],
        }

    def index(self, place):
        return sum(((lax.axis_index(axis) >> k) & 1) << shift for (axis, k), shift in place.items())

    def swap(self, block, bit):
        axis, k = bit
        return lax.ppermute(block, axis, [(i, i ^ (1 << k)) for i in range(self.sizes[axis])])

    def offsets(self, order, place):
        last = len(order) - 1
        return [
            sum(1 << place[bit] for k, bit in enumerate(order) if (p >> (last - k)) & 1)
            for p in range(1 << len(order))
        ]

    def spread(self, held, bits):
        for bit in bits:
            held = jnp.concatenate([held, (yield held, bit)], axis=0)
        return held

    def gather(self, held, order):
        done = held.shape[0].bit_length() - 1
        held = yield from self.spread(held, order[:0:-1][done:])
        return held, (yield held, order[0])

    def natural(self, halves, order, segments, place):
        low, high = halves
        offsets = self.offsets(order, place)
        count, half = 2 * low.shape[0], low.shape[0]
        columns = low.shape[2]
        starts = [sum(segments[:k]) for k in range(len(segments))]
        index = self.index(place)
        if any(rows % 16 for rows in segments):
            where = np.argsort(np.array(offsets))
            picked = jnp.asarray(where)[jnp.arange(count) ^ index]
            blocks = jnp.take(jnp.concatenate(halves, axis=0), picked, axis=0)
            return [
                blocks[:, start : start + rows].reshape(count * rows, columns)
                for start, rows in zip(starts, segments)
            ]
        pieces = list(enumerate(zip(starts, segments)))

        def body(index_ref, low_ref, high_ref, *refs):
            index, sems = index_ref[0], refs[-1]
            copies = []
            for p in range(count):
                source = low_ref.at[p] if p < half else high_ref.at[p - half]
                for k, (start, rows) in pieces:
                    copies.append(
                        pltpu.make_async_copy(
                            source.at[pl.ds(start, rows)], refs[k].at[index ^ offsets[p]], sems.at[p, k]
                        )
                    )
                    copies[-1].start()
            for copy in copies:
                copy.wait()

        moved = pl.pallas_call(
            body,
            out_shape=[jax.ShapeDtypeStruct((count, rows, columns), low.dtype) for rows in segments],
            in_specs=[
                pl.BlockSpec(memory_space=pltpu.SMEM),
                pl.BlockSpec(memory_space=pl.ANY),
                pl.BlockSpec(memory_space=pl.ANY),
            ],
            out_specs=[pl.BlockSpec(memory_space=pltpu.VMEM) for _ in segments],
            scratch_shapes=[pltpu.SemaphoreType.DMA((count, len(segments)))],
            compiler_params=pltpu.CompilerParams(vmem_limit_bytes=40 * 2**20),
            name="natural_order",
        )(index.astype(jnp.int32).reshape(1), low, high)
        return [block.reshape(count * rows, columns) for block, rows in zip(moved, segments)]

    def unpacked(self, packed):
        rows, columns = packed.shape[1] // (self.count // 2), packed.shape[2]
        count, far, half = self.count // 2, self.far, columns // 2

        def widen(blocks):
            return blocks.reshape(2, far, -1, columns).transpose(1, 0, 2, 3).reshape(-1, columns)

        if rows % 16:
            narrow = packed[2:].reshape(2, count, rows, 2, half).transpose(1, 3, 0, 2, 4)
            return widen(packed[:2]), narrow.reshape(-1, half)

        def body(packed_ref, widen_ref, narrow_ref, sems):
            copies = [pltpu.make_async_copy(packed_ref.at[pl.ds(0, 2)], widen_ref, sems.at[0])]
            for p in range(count):
                for k in range(4):
                    source = packed_ref.at[
                        2 + k % 2, pl.ds(p * rows, rows), pl.ds((k // 2) * half, half)
                    ]
                    copies.append(
                        pltpu.make_async_copy(
                            source, narrow_ref.at[p, pl.ds(k * rows, rows)], sems.at[1 + 4 * p + k]
                        )
                    )
            for copy in copies:
                copy.start()
            for copy in copies:
                copy.wait()

        wide, narrow = pl.pallas_call(
            body,
            out_shape=[
                jax.ShapeDtypeStruct((2, count * rows, columns), packed.dtype),
                jax.ShapeDtypeStruct((count, 4 * rows, half), packed.dtype),
            ],
            in_specs=[pl.BlockSpec(memory_space=pl.ANY)],
            out_specs=[pl.BlockSpec(memory_space=pltpu.VMEM)] * 2,
            scratch_shapes=[pltpu.SemaphoreType.DMA((1 + 4 * count,))],
            compiler_params=pltpu.CompilerParams(vmem_limit_bytes=40 * 2**20),
            name="unpacked",
        )(packed)
        return widen(wide), narrow.reshape(-1, half)

    def turned(self, sources, orders, place):
        tokens, features = sources[0].shape
        count = 1 << len(place)
        rows, wide = features // count, tokens * len(sources)
        tables = [self.offsets(order, place) for order in orders]
        index = self.index(place)
        if rows % 16:
            blocks = jnp.concatenate(sources, axis=0).T.reshape(count, rows, wide)
            return [jnp.take(blocks, jnp.asarray(table) ^ index, axis=0) for table in tables]

        def body(index_ref, *refs):
            index = index_ref[0]
            ins, outs, held = refs[: len(sources)], refs[len(sources) : -1], refs[-1]
            for k, in_ref in enumerate(ins):
                held[:, :, pl.ds(k * tokens, tokens)] = in_ref[...].T.reshape(count, rows, tokens)
            for table, out in zip(tables, outs):
                for p in range(count):
                    out[p] = held[index ^ table[p]]

        shape = (count, rows, wide)
        return pl.pallas_call(
            body,
            out_shape=[jax.ShapeDtypeStruct(shape, sources[0].dtype) for _ in tables],
            in_specs=[pl.BlockSpec(memory_space=pltpu.SMEM)]
            + [pl.BlockSpec(memory_space=pltpu.VMEM) for _ in sources],
            out_specs=[pl.BlockSpec(memory_space=pltpu.VMEM) for _ in tables],
            scratch_shapes=[pltpu.VMEM(shape, sources[0].dtype)],
            compiler_params=pltpu.CompilerParams(vmem_limit_bytes=40 * 2**20),
            name="turned",
        )(index.astype(jnp.int32).reshape(1), *sources)

    def scatter(self, sides, order, extra=None):
        blocks = 1 << len(order)
        half, quarter = blocks // 2, blocks // 4

        def parts(first, last, got=None):
            terms, column = [], 0
            for turned, other in sides:
                rows = turned.shape[0] // blocks
                block = turned[first * rows : last * rows]
                term = product(block.reshape(-1, turned.shape[-1]), other)
                if got is not None:
                    term = term + got[:, column : column + term.shape[1]].astype(jnp.float32)
                column += term.shape[1]
                terms.append(term)
            if extra is not None:
                rows = extra.shape[0] // blocks
                term = extra[first * rows : last * rows]
                if got is not None:
                    term = term + got[:, column:].astype(jnp.float32)
                terms.append(term)
            return terms

        def joined(terms):
            return terms[0] if len(terms) == 1 else jnp.concatenate(terms, axis=1)

        got = yield joined([rounded(term) for term in parts(half, blocks)]), order[0]
        middle = got.shape[0] // 2
        sent = joined([rounded(term) for term in parts(quarter, half, got[middle:])])
        kept = joined(parts(0, quarter, got[:middle]))
        for bit in order[1:-1]:
            got = yield sent, bit
            middle = kept.shape[0] // 2
            sent = rounded(kept[middle:] + got[middle:].astype(jnp.float32))
            kept = kept[:middle] + got[:middle].astype(jnp.float32)
        return kept + (yield sent, order[-1]).astype(jnp.float32)

    def scatter_pair(self, sides, order):
        kept = yield from self.scatter(sides, order)
        middle = kept.shape[0] // 2
        got = (yield rounded(kept[middle:]), PAIR).astype(jnp.float32)
        return kept[:middle], got


class Driver:
    def __init__(self, cube, depth):
        self.cube, self.depth = cube, depth
        self.before = {bit: [] for bit in cube.place}
        self.chains, self.got, self.results = {}, {}, {}
        self.token = None
        self.starts, self.calls = {}, {}

    def swap(self, block, bit):
        past = self.before[bit]
        if len(past) >= self.depth:
            block, _ = lax.optimization_barrier((block, past[-self.depth]))
        past.append(self.cube.swap(block, bit))
        return past[-1]

    def after(self, block):
        if self.token is None:
            return block
        return lax.optimization_barrier((block, self.token))[0]

    def done(self, block):
        self.token = block
        return block

    def add(self, name, chain):
        self.chains[name] = chain
        block, bit = next(chain)
        self.token = block
        self.got[name] = self.swap(block, bit)

    def advance(self, names):
        for name in names:
            if name in self.calls:
                self.results[name] = self.calls.pop(name)()
                continue
            if name in self.starts:
                self.add(name, self.starts.pop(name)())
                continue
            if name in self.results:
                continue
            got = self.after(self.got[name])
            try:
                block, bit = self.chains[name].send(got)
            except StopIteration as stop:
                self.results[name] = stop.value
                self.token = got
                continue
            self.token = block
            self.got[name] = self.swap(block, bit)

    def finish(self, names):
        while left := [name for name in names if name not in self.results]:
            self.advance(left)
        return [self.results[name] for name in names]


def per_device(
    cube,
    tokens,
    memory,
    token_segments,
    memory_segments,
    padding,
    self_project,
    self_output,
    cross_project,
    cross_output,
    widen_weight,
    narrow_weight,
    norm_gain,
    norm_bias,
    grad_out,
):
    token_low = tokens[0]
    memory_low = memory[0]
    row_in = token_low.astype(jnp.float32)
    segment_row = token_segments[0]
    places = jnp.arange(segment_row.shape[0])
    diagonal = places[None, :] == places[:, None]
    live_keys = padding[0] == 1
    self_allowed = (
        (segment_row[:, None] == segment_row[None, :])
        & (places[None, :] <= places[:, None])
        & (live_keys[None, :] | diagonal)
    )
    cross_allowed = segment_row[:, None] == memory_segments[0][None, :]
    pad_scale = padding[0].astype(jnp.float32)[:, None]
    width = token_low.shape[1]
    own = self_project.shape[1]
    hidden_width = widen_weight.shape[1]
    count, far = cube.count, cube.far
    orders = cube.orders
    side = lax.axis_index("pair")
    drive = Driver(cube, GATHER_DEPTH)

    def both_sides(mine, other):
        return [jnp.where(side == 0, mine, other), jnp.where(side == 0, other, mine)]

    shard = widen_weight.reshape(own, far, 2, hidden_width // (2 * far))
    mine, other = (
        lax.dynamic_index_in_dim(shard, k, axis=2, keepdims=False).reshape(own, hidden_width // 2)
        for k in (side, 1 - side)
    )
    narrow_shard = jnp.concatenate([narrow_weight[: 2 * own], narrow_weight[2 * own :]], axis=1)
    wide_shard = jnp.concatenate(
        [*both_sides(mine, drive.swap(other, PAIR)), narrow_shard], axis=0
    ).reshape(4, own, 2 * width)

    def gather_wide():
        return lax.all_gather(drive.after(wide_shard), ("far", "core", "fsdp"), axis=1, tiled=True)

    def gather_cross():
        return lax.all_gather(drive.after(cross_project[1:]), AXES, axis=1, tiled=True)

    norm_rows = jnp.concatenate([norm_gain, norm_bias], axis=0)
    norm_rows = jnp.pad(norm_rows, ((0, 16 - 6), (0, width - own)))
    shared = orders["A"][:2:-1]
    self_shard = jnp.concatenate([self_project.reshape(3 * own, width), self_output, norm_rows], axis=0)
    cross_shard = jnp.concatenate([cross_project[0], cross_output], axis=0)
    drive.calls = {"wide": gather_wide, "cross": gather_cross}
    drive.starts = {
        "s": lambda: cube.spread(self_shard[None], shared),
        "c": lambda: cube.spread(cross_shard[None], shared),
        "s1": lambda: cube.gather(drive.finish(["s"])[0][:, : 2 * own], orders[GATHER["s1"]]),
        "s2": lambda: cube.gather(drive.finish(["s"])[0][:, 2 * own :], orders[GATHER["s2"]]),
        "c1": lambda: cube.gather(drive.finish(["c"])[0][:, :own], orders[GATHER["c1"]]),
        "c2": lambda: cube.gather(drive.finish(["c"])[0][:, own:], orders[GATHER["c2"]]),
    }
    drive.advance(STEPS["early"])
    drive.finish(["s", "c"])
    drive.advance(STEPS["self"])
    drive.finish(["s1", "s2"])
    query_full, key_full = cube.natural(drive.results["s1"], orders[GATHER["s1"]], [own, own], cube.place)
    value_full, self_final, norms = cube.natural(drive.results["s2"], orders[GATHER["s2"]], [own, own, 16], cube.place)
    self_stack = [query_full, key_full, value_full]
    norms = norms.reshape(count, 16, width)[:, :6, :own].transpose(1, 0, 2).reshape(6, width)
    norms = norms.astype(jnp.float32)
    gain_values, bias_values = norms[:3], norms[3:]

    self_query, self_key, self_value = project_three(token_low, token_low, self_stack)
    self_mixed, self_logsum = attend_forward(self_query, self_key, self_value, self_allowed)
    pre_one = ALPHA * row_in + product(self_mixed, self_final)
    first_out = normalize(pre_one, gain_values[0], bias_values[0])
    first_low = rounded(first_out)

    drive.done(first_low)
    drive.advance(STEPS["cross"])
    drive.finish(["c1", "c2"])
    drive.finish(["wide", "cross"])
    (query_full,) = cube.natural(drive.results["c1"], orders[GATHER["c1"]], [own], cube.place)
    (cross_final,) = cube.natural(drive.results["c2"], orders[GATHER["c2"]], [own], cube.place)
    cross_stack = [query_full, *drive.results["cross"]]
    cross_query, cross_key, cross_value = project_three(first_low, memory_low, cross_stack)
    cross_mixed, cross_logsum = attend_forward(cross_query, cross_key, cross_value, cross_allowed)
    pre_two = ALPHA * first_out + product(cross_mixed, cross_final)
    second = normalize(pre_two, gain_values[1], bias_values[1])
    second_low = rounded(second)

    widen_full, narrow_full = cube.unpacked(drive.results["wide"])

    def widened(rows_low):
        hidden = product(rows_low, widen_full)
        active = rounded(jax.nn.gelu(hidden))
        return hidden, active, product(active, narrow_full)

    second_other = cube.swap(second_low, PAIR)
    hidden, active, branch = widened(second_low)
    hidden_other, active_other, branch_other = widened(second_other)
    branch_got = cube.swap(rounded(branch_other), PAIR)
    pre_three = ALPHA * second + (branch + branch_got.astype(jnp.float32))
    third_out = normalize(pre_three, gain_values[2], bias_values[2])
    layer_out = rounded(third_out * pad_scale)

    (self_mixed_turned,) = cube.turned([self_mixed], [orders[SCATTER["S2"]]], cube.place)
    token_turned = cube.turned([token_low], [orders[SCATTER["S1"]], orders[SCATTER["S2"]]], cube.place)
    (first_turned,) = cube.turned([first_low], [orders[SCATTER["P2"]]], cube.place)
    (memory_turned,) = cube.turned([memory_low], [orders[SCATTER["P1"]]], cube.place)
    (cross_mixed_turned,) = cube.turned([cross_mixed], [orders[SCATTER["P2"]]], cube.place)
    (second_turned,) = cube.turned([second_low, second_other], [[*orders[SCATTER["W"]], PAIR]], cube.place)
    (active_turned,) = cube.turned([active, active_other], [orders[SCATTER["N"]]], cube.side_place)
    drive = Driver(cube, SCATTER_DEPTH)

    grad_third = grad_out[0].astype(jnp.float32) * pad_scale
    grad_pre_three, grad_gain_three, grad_bias_three = normalize_back(
        pre_three, gain_values[2], bias_values[2], grad_third
    )
    ffn_branch = rounded(grad_pre_three)

    def widened_back(branch_low, hidden):
        grad_active = product(branch_low, narrow_full.T)
        unused, gelu_pull = jax.vjp(jax.nn.gelu, hidden)
        grad_hidden = rounded(gelu_pull(grad_active)[0])
        return grad_hidden, product(grad_hidden, widen_full.T)

    ffn_branch_other = cube.swap(ffn_branch, PAIR)
    grad_hidden, grad_branch = widened_back(ffn_branch, hidden)
    grad_hidden_other, grad_branch_other = widened_back(ffn_branch_other, hidden_other)
    grad_branch_got = drive.swap(drive.done(rounded(grad_branch_other)), PAIR)
    drive.add(
        "N",
        cube.scatter(
            [(drive.after(active_turned), jnp.concatenate([ffn_branch, ffn_branch_other], axis=0))], orders[SCATTER["N"]]
        ),
    )
    drive.add(
        "W",
        cube.scatter_pair(
            [(drive.after(second_turned), jnp.concatenate([grad_hidden, grad_hidden_other], axis=0))],
            orders[SCATTER["W"]],
        ),
    )
    grad_branch_got = drive.after(grad_branch_got)
    grad_second = ALPHA * grad_pre_three + (grad_branch + grad_branch_got.astype(jnp.float32))

    grad_pre_two, grad_gain_two, grad_bias_two = normalize_back(
        pre_two, gain_values[1], bias_values[1], grad_second
    )
    cross_branch = drive.done(rounded(grad_pre_two))
    drive.advance(STEPS["gs"])
    cross_branch = drive.after(cross_branch)
    grad_mixed = rounded(product(cross_branch, cross_final.T))
    cross_keys, cross_dq = attend_backward(
        cross_query, cross_key, cross_value, cross_allowed, cross_logsum, grad_mixed, (("k", "v"), ("q",))
    )
    cross_dk, cross_dv = cross_keys[:, :width], cross_keys[:, width:]
    grad_first_in, grad_memory = project_inputs(cross_stack, cross_dq, cross_dk, cross_dv)
    grad_first = ALPHA * grad_pre_two + grad_first_in
    drive.add(
        "P1",
        cube.scatter([(memory_turned, cross_keys)], orders[SCATTER["P1"]]),
    )
    drive.add(
        "P2",
        cube.scatter([(first_turned, cross_dq), (cross_mixed_turned, cross_branch)], orders[SCATTER["P2"]]),
    )
    drive.advance(STEPS["gf"])
    grad_first = drive.after(grad_first)

    grad_pre_one, grad_gain_one, grad_bias_one = normalize_back(
        pre_one, gain_values[0], bias_values[0], grad_first
    )
    self_branch = rounded(grad_pre_one)
    grad_mixed = rounded(product(self_branch, self_final.T))
    self_keys, self_dv = attend_backward(
        self_query, self_key, self_value, self_allowed, self_logsum, grad_mixed, (("q", "k"), ("v",))
    )
    self_dq, self_dk = self_keys[:, :width], self_keys[:, width:]
    grad_norms = jnp.stack(
        [
            grad_gain_one,
            grad_gain_two,
            grad_gain_three,
            grad_bias_one,
            grad_bias_two,
            grad_bias_three,
        ]
    )
    grad_norms = jnp.pad(lax.optimization_barrier(grad_norms), ((0, 128 - 6), (0, 0)))
    (norms_turned,) = cube.turned([grad_norms], [orders[SCATTER["S2"]]], cube.place)
    drive.advance(STEPS["pre"])
    drive.add(
        "S1",
        cube.scatter(
            [(drive.after(token_turned[0]), self_keys)], orders[SCATTER["S1"]]
        ),
    )
    drive.add(
        "S2",
        cube.scatter(
            [(drive.after(token_turned[1]), self_dv), (self_mixed_turned, self_branch)],
            orders[SCATTER["S2"]],
            norms_turned.reshape(width, 128),
        ),
    )
    grad_query_in, grad_key_in = project_inputs(self_stack, drive.after(self_dq), self_dk, self_dv)
    grad_tokens = ALPHA * grad_pre_one + grad_query_in + grad_key_in
    drive.advance(STEPS["tail"])
    drive.finish(["N", "W", "P1", "P2", "S1", "S2"])
    sums = drive.results
    grad_norms = sums["S2"][:, 2 * width : 2 * width + 6].T
    widen_mine, widen_other = sums["W"]
    grad_widen = jnp.stack(
        [
            block.reshape(own, far, hidden_width // (2 * far))
            for block in both_sides(widen_mine, widen_other)
        ],
        axis=2,
    ).reshape(own, hidden_width)
    return (
        layer_out[None],
        grad_tokens[None],
        grad_memory[None],
        jnp.stack([sums["S1"][:, :width], sums["S1"][:, width:], sums["S2"][:, :width]]),
        sums["S2"][:, width : 2 * width],
        jnp.stack([sums["P2"][:, :width], sums["P1"][:, :width], sums["P1"][:, width:]]),
        sums["P2"][:, width:],
        grad_widen,
        sums["N"],
        grad_norms[:3],
        grad_norms[3:],
    )


def solution(mesh):
    cube = Cube(mesh)
    return jax.shard_map(
        functools.partial(per_device, cube),
        mesh=cube.mesh,
        in_specs=(
            P(AXES, None, None),
            P(AXES, None, None),
            P(AXES, None),
            P(AXES, None),
            P(AXES, None),
            P(None, AXES, None),
            P(AXES, None),
            P(None, AXES, None),
            P(AXES, None),
            P(AXES, None),
            P(AXES, None),
            P(None, AXES),
            P(None, AXES),
            P(AXES, None, None),
        ),
        out_specs=(
            P(AXES, None, None),
            P(AXES, None, None),
            P(AXES, None, None),
            P(None, AXES, None),
            P(AXES, None),
            P(None, AXES, None),
            P(AXES, None),
            P(AXES, None),
            P(AXES, None),
            P(None, AXES),
            P(None, AXES),
        ),
        check_vma=False,
    )
```

```python
import functools

import jax
import jax.numpy as jnp
import numpy as np
from jax import lax
from jax.experimental import pallas as pl
from jax.experimental.pallas import tpu as pltpu
from jax.sharding import PartitionSpec as P

HEADS = 16
HEAD = 64


ALPHA = (3.0 * 200.0) ** 0.25
EPSILON = 1e-05
MASKED = -1e30


def rounded(values_in):
    return values_in.astype(jnp.bfloat16)


def product(first_side, other_side):
    return jnp.dot(first_side, other_side, preferred_element_type=jnp.float32)


AXES = ("far", "pair", "core", "fsdp")
PAIR = ("pair", 0)
CORE = ("core", 0)
GATHER_DEPTH = 2
SCATTER_DEPTH = 4
GATHER = {"s1": "A", "s2": "B", "c1": "A", "c2": "B"}
SCATTER = {"N": "E", "W": "F", "P1": "B", "P2": "D", "S1": "A", "S2": "B"}
STEPS = {
    "gs": ["W", "N"],
    "gf": ["P2", "P1", "W", "N"],
    "pre": ["P2", "P1"],
    "tail": ["S1", "S2", "W", "N", "P2", "P1", "S1", "S2", "W", "N", "P2", "P1", "S2", "S1", "W", "P2", "P1", "S2", "S1", "S2", "S1"],
    "early": ["s", "cross", "s", "c", "s", "s1", "s2", "c"],
    "self": ["s1", "s2", "c", "wide", "c1", "c2", "s1", "s2", "c1", "c2", "s1", "s2"],
    "cross": ["c1", "c2", "c1", "c2"],
    "mid": [],
}


def normalize(values_in, scale_row, shift_row):
    average = jnp.mean(values_in, axis=-1, keepdims=True)
    centred = values_in - average
    spread = jnp.mean(centred * centred, axis=-1, keepdims=True)
    return centred * lax.rsqrt(spread + EPSILON) * scale_row + shift_row


def normalize_back(values_in, scale_row, shift_row, grad_result):
    unused, pullback = jax.vjp(normalize, values_in, scale_row, shift_row)
    return pullback(grad_result)


def project_three(query_source, key_source, weight_stack):
    return (
        rounded(product(query_source, weight_stack[0])),
        rounded(product(key_source, weight_stack[1])),
        rounded(product(key_source, weight_stack[2])),
    )


def project_inputs(weight_stack, grad_query, grad_key, grad_value):
    grad_query_side = product(grad_query, weight_stack[0].T)
    grad_key_side = product(grad_key, weight_stack[1].T) + product(grad_value, weight_stack[2].T)
    return (grad_query_side, grad_key_side)


def attend_forward(queries, key_rows, values, allowed):
    length, width = queries.shape
    lanes = 2 * HEAD

    def body(q_ref, k_ref, v_ref, allowed_ref, mixed_ref, logsum_ref):
        kept = allowed_ref[...] > 0.0
        lane = lax.broadcasted_iota(jnp.int32, (1, lanes), 1)
        for pair in range(width // lanes):
            columns = pl.ds(pair * lanes, lanes)
            query, key_block, value = (ref[:, columns] for ref in (q_ref, k_ref, v_ref))
            mixed = 0.0
            for half in range(2):
                head = 2 * pair + half
                here = ((lane // HEAD) == half).astype(jnp.float32).astype(jnp.bfloat16)
                scores = across(query * here, key_block, 1, 1) * HEAD ** (-0.5)
                scores = jnp.where(kept, scores, MASKED)
                largest = jnp.max(scores, axis=-1, keepdims=True)
                exponentials = jnp.exp(scores - largest)
                totals = jnp.sum(exponentials, axis=-1, keepdims=True)
                mixed += across(rounded(exponentials / totals), value * here, 1, 0)
                logsum_ref[:, head : head + 1] = largest + jnp.log(totals)
            mixed_ref[:, columns] = rounded(mixed)

    vmem = pl.BlockSpec(memory_space=pltpu.VMEM)
    return pl.pallas_call(
        body,
        out_shape=[
            jax.ShapeDtypeStruct((length, width), queries.dtype),
            jax.ShapeDtypeStruct((length, width // HEAD), jnp.float32),
        ],
        in_specs=[vmem] * 4,
        out_specs=[vmem] * 2,
        compiler_params=pltpu.CompilerParams(vmem_limit_bytes=40 * 2**20),
        cost_estimate=pl.CostEstimate(flops=1, bytes_accessed=1, transcendentals=0),
        name="attend_forward",
    )(queries, key_rows, values, allowed.astype(jnp.float32))


def attend_backward(queries, key_rows, values, allowed, logsum, grad_mixed, groups):
    length, width = queries.shape
    key_count, lanes = key_rows.shape[0], 2 * HEAD
    heights = {"q": length, "k": key_count, "v": key_count}

    def body(q_ref, k_ref, v_ref, grad_ref, allowed_ref, logsum_ref, *outs):
        kept = allowed_ref[...] > 0.0
        lane = lax.broadcasted_iota(jnp.int32, (1, lanes), 1)
        for pair in range(width // lanes):
            columns = pl.ds(pair * lanes, lanes)
            query, key_block, value, grad = (
                ref[:, columns] for ref in (q_ref, k_ref, v_ref, grad_ref)
            )
            totals = {"q": 0.0, "k": 0.0, "v": 0.0}
            for half in range(2):
                head = 2 * pair + half
                here = ((lane // HEAD) == half).astype(jnp.float32).astype(jnp.bfloat16)
                query_half, key_half, grad_half = query * here, key_block * here, grad * here
                scores = across(query_half, key_block, 1, 1) * HEAD ** (-0.5)
                weights = jnp.exp(jnp.where(kept, scores, MASKED) - logsum_ref[:, head : head + 1])
                grad_weights = across(grad_half, value, 1, 1)
                inner_sum = jnp.sum(weights * grad_weights, axis=-1, keepdims=True)
                grad_scores = rounded(weights * (grad_weights - inner_sum))
                totals["q"] += across(grad_scores, key_half, 1, 0)
                totals["k"] += across(grad_scores, query_half, 0, 0)
                totals["v"] += across(rounded(weights), grad_half, 0, 0)
            totals["q"] *= HEAD ** (-0.5)
            totals["k"] *= HEAD ** (-0.5)
            for group, out in zip(groups, outs):
                for k, name in enumerate(group):
                    out[:, pl.ds(k * width + pair * lanes, lanes)] = rounded(totals[name])

    vmem = pl.BlockSpec(memory_space=pltpu.VMEM)
    return pl.pallas_call(
        body,
        out_shape=[
            jax.ShapeDtypeStruct((heights[group[0]], len(group) * width), queries.dtype) for group in groups
        ],
        in_specs=[vmem] * 6,
        out_specs=[vmem for _ in groups],
        compiler_params=pltpu.CompilerParams(vmem_limit_bytes=40 * 2**20),
        cost_estimate=pl.CostEstimate(flops=1, bytes_accessed=1, transcendentals=0),
        name="attend_backward",
    )(
        queries,
        key_rows,
        values,
        grad_mixed,
        allowed.astype(jnp.float32),
        logsum,
    )


def across(one, other, one_dim, other_dim):
    return lax.dot_general(
        one, other, (((one_dim,), (other_dim,)), ((), ())), preferred_element_type=jnp.float32
    )


class Cube:
    def __init__(self, mesh):
        far, inner = mesh.shape["dp"] // 4, mesh.shape["fsdp"]
        self.mesh = jax.sharding.Mesh(mesh.devices.reshape(far, 2, 2, inner), AXES)
        self.sizes = dict(zip(AXES, (far, 2, 2, inner)))
        self.count = 4 * far * inner
        self.far = far
        close = [("fsdp", k) for k in range(inner.bit_length() - 1)]
        apart = [("far", k) for k in range(far.bit_length() - 1)]
        self.place = {bit: k for k, bit in enumerate([*close, CORE, PAIR, *apart])}
        self.side_place = {bit: k for k, bit in enumerate([*close, CORE, *apart])}
        self.orders = {
            "A": [CORE, close[0], PAIR, *close[1:], *apart],
            "B": [CORE, PAIR, *close, *apart],
            "C": [CORE, close[1], close[0], PAIR, *close[2:], *apart],
            "D": [CORE, close[1], PAIR, close[0], *close[2:], *apart],
            "E": [CORE, *close, *apart],
            "F": [CORE, close[1], close[0], *close[2:], *apart],
            "H": [CORE, *close[1:], close[0], *apart],
        }

    def index(self, place):
        return sum(((lax.axis_index(axis) >> k) & 1) << shift for (axis, k), shift in place.items())

    def swap(self, block, bit):
        axis, k = bit
        return lax.ppermute(block, axis, [(i, i ^ (1 << k)) for i in range(self.sizes[axis])])

    def offsets(self, order, place):
        last = len(order) - 1
        return [
            sum(1 << place[bit] for k, bit in enumerate(order) if (p >> (last - k)) & 1)
            for p in range(1 << len(order))
        ]

    def spread(self, held, bits):
        for bit in bits:
            held = jnp.concatenate([held, (yield held, bit)], axis=0)
        return held

    def gather(self, held, order):
        done = held.shape[0].bit_length() - 1
        held = yield from self.spread(held, order[:0:-1][done:])
        return held, (yield held, order[0])

    def natural(self, halves, order, segments, place):
        low, high = halves
        offsets = self.offsets(order, place)
        count, half = 2 * low.shape[0], low.shape[0]
        columns = low.shape[2]
        starts = [sum(segments[:k]) for k in range(len(segments))]
        index = self.index(place)
        if any(rows % 16 for rows in segments):
            where = np.argsort(np.array(offsets))
            picked = jnp.asarray(where)[jnp.arange(count) ^ index]
            blocks = jnp.take(jnp.concatenate(halves, axis=0), picked, axis=0)
            return [
                blocks[:, start : start + rows].reshape(count * rows, columns)
                for start, rows in zip(starts, segments)
            ]
        pieces = list(enumerate(zip(starts, segments)))

        def body(index_ref, low_ref, high_ref, *refs):
            index, sems = index_ref[0], refs[-1]
            copies = []
            for p in range(count):
                source = low_ref.at[p] if p < half else high_ref.at[p - half]
                for k, (start, rows) in pieces:
                    copies.append(
                        pltpu.make_async_copy(
                            source.at[pl.ds(start, rows)], refs[k].at[index ^ offsets[p]], sems.at[p, k]
                        )
                    )
                    copies[-1].start()
            for copy in copies:
                copy.wait()

        moved = pl.pallas_call(
            body,
            out_shape=[jax.ShapeDtypeStruct((count, rows, columns), low.dtype) for rows in segments],
            in_specs=[
                pl.BlockSpec(memory_space=pltpu.SMEM),
                pl.BlockSpec(memory_space=pl.ANY),
                pl.BlockSpec(memory_space=pl.ANY),
            ],
            out_specs=[pl.BlockSpec(memory_space=pltpu.VMEM) for _ in segments],
            scratch_shapes=[pltpu.SemaphoreType.DMA((count, len(segments)))],
            compiler_params=pltpu.CompilerParams(vmem_limit_bytes=40 * 2**20),
            name="natural_order",
        )(index.astype(jnp.int32).reshape(1), low, high)
        return [block.reshape(count * rows, columns) for block, rows in zip(moved, segments)]

    def unpacked(self, packed):
        rows, columns = packed.shape[1] // (self.count // 2), packed.shape[2]
        count, far, half = self.count // 2, self.far, columns // 2

        def widen(blocks):
            return blocks.reshape(2, far, -1, columns).transpose(1, 0, 2, 3).reshape(-1, columns)

        if rows % 16:
            narrow = packed[2:].reshape(2, count, rows, 2, half).transpose(1, 3, 0, 2, 4)
            return widen(packed[:2]), narrow.reshape(-1, half)

        def body(packed_ref, widen_ref, narrow_ref, sems):
            copies = [pltpu.make_async_copy(packed_ref.at[pl.ds(0, 2)], widen_ref, sems.at[0])]
            for p in range(count):
                for k in range(4):
                    source = packed_ref.at[
                        2 + k % 2, pl.ds(p * rows, rows), pl.ds((k // 2) * half, half)
                    ]
                    copies.append(
                        pltpu.make_async_copy(
                            source, narrow_ref.at[p, pl.ds(k * rows, rows)], sems.at[1 + 4 * p + k]
                        )
                    )
            for copy in copies:
                copy.start()
            for copy in copies:
                copy.wait()

        wide, narrow = pl.pallas_call(
            body,
            out_shape=[
                jax.ShapeDtypeStruct((2, count * rows, columns), packed.dtype),
                jax.ShapeDtypeStruct((count, 4 * rows, half), packed.dtype),
            ],
            in_specs=[pl.BlockSpec(memory_space=pl.ANY)],
            out_specs=[pl.BlockSpec(memory_space=pltpu.VMEM)] * 2,
            scratch_shapes=[pltpu.SemaphoreType.DMA((1 + 4 * count,))],
            compiler_params=pltpu.CompilerParams(vmem_limit_bytes=40 * 2**20),
            name="unpacked",
        )(packed)
        return widen(wide), narrow.reshape(-1, half)

    def turned(self, sources, orders, place):
        tokens, features = sources[0].shape
        count = 1 << len(place)
        rows, wide = features // count, tokens * len(sources)
        tables = [self.offsets(order, place) for order in orders]
        index = self.index(place)
        if rows % 16:
            blocks = jnp.concatenate(sources, axis=0).T.reshape(count, rows, wide)
            return [jnp.take(blocks, jnp.asarray(table) ^ index, axis=0) for table in tables]

        def body(index_ref, *refs):
            index = index_ref[0]
            ins, outs, held = refs[: len(sources)], refs[len(sources) : -1], refs[-1]
            for k, in_ref in enumerate(ins):
                held[:, :, pl.ds(k * tokens, tokens)] = in_ref[...].T.reshape(count, rows, tokens)
            for table, out in zip(tables, outs):
                for p in range(count):
                    out[p] = held[index ^ table[p]]

        shape = (count, rows, wide)
        return pl.pallas_call(
            body,
            out_shape=[jax.ShapeDtypeStruct(shape, sources[0].dtype) for _ in tables],
            in_specs=[pl.BlockSpec(memory_space=pltpu.SMEM)]
            + [pl.BlockSpec(memory_space=pltpu.VMEM) for _ in sources],
            out_specs=[pl.BlockSpec(memory_space=pltpu.VMEM) for _ in tables],
            scratch_shapes=[pltpu.VMEM(shape, sources[0].dtype)],
            compiler_params=pltpu.CompilerParams(vmem_limit_bytes=40 * 2**20),
            name="turned",
        )(index.astype(jnp.int32).reshape(1), *sources)

    def scatter(self, sides, order, extra=None):
        blocks = 1 << len(order)
        half, quarter = blocks // 2, blocks // 4

        def parts(first, last, got=None):
            terms, column = [], 0
            for turned, other in sides:
                rows = turned.shape[0] // blocks
                block = turned[first * rows : last * rows]
                term = product(block.reshape(-1, turned.shape[-1]), other)
                if got is not None:
                    term = term + got[:, column : column + term.shape[1]].astype(jnp.float32)
                column += term.shape[1]
                terms.append(term)
            if extra is not None:
                rows = extra.shape[0] // blocks
                term = extra[first * rows : last * rows]
                if got is not None:
                    term = term + got[:, column:].astype(jnp.float32)
                terms.append(term)
            return terms

        def joined(terms):
            return terms[0] if len(terms) == 1 else jnp.concatenate(terms, axis=1)

        got = yield joined([rounded(term) for term in parts(half, blocks)]), order[0]
        middle = got.shape[0] // 2
        sent = joined([rounded(term) for term in parts(quarter, half, got[middle:])])
        kept = joined(parts(0, quarter, got[:middle]))
        for bit in order[1:-1]:
            got = yield sent, bit
            middle = kept.shape[0] // 2
            sent = rounded(kept[middle:] + got[middle:].astype(jnp.float32))
            kept = kept[:middle] + got[:middle].astype(jnp.float32)
        return kept + (yield sent, order[-1]).astype(jnp.float32)

    def scatter_pair(self, sides, order):
        kept = yield from self.scatter(sides, order)
        middle = kept.shape[0] // 2
        got = (yield rounded(kept[middle:]), PAIR).astype(jnp.float32)
        return kept[:middle], got


class Driver:
    def __init__(self, cube, depth):
        self.cube, self.depth = cube, depth
        self.before = {bit: [] for bit in cube.place}
        self.chains, self.got, self.results = {}, {}, {}
        self.token = None
        self.starts, self.calls = {}, {}

    def swap(self, block, bit):
        past = self.before[bit]
        if len(past) >= self.depth:
            block, _ = lax.optimization_barrier((block, past[-self.depth]))
        past.append(self.cube.swap(block, bit))
        return past[-1]

    def after(self, block):
        if self.token is None:
            return block
        return lax.optimization_barrier((block, self.token))[0]

    def done(self, block):
        self.token = block
        return block

    def add(self, name, chain):
        self.chains[name] = chain
        block, bit = next(chain)
        self.token = block
        self.got[name] = self.swap(block, bit)

    def advance(self, names):
        for name in names:
            if name in self.calls:
                self.results[name] = self.calls.pop(name)()
                continue
            if name in self.starts:
                self.add(name, self.starts.pop(name)())
                continue
            if name in self.results:
                continue
            got = self.after(self.got[name])
            try:
                block, bit = self.chains[name].send(got)
            except StopIteration as stop:
                self.results[name] = stop.value
                self.token = got
                continue
            self.token = block
            self.got[name] = self.swap(block, bit)

    def finish(self, names):
        while left := [name for name in names if name not in self.results]:
            self.advance(left)
        return [self.results[name] for name in names]


def per_device(
    cube,
    tokens,
    memory,
    token_segments,
    memory_segments,
    padding,
    self_project,
    self_output,
    cross_project,
    cross_output,
    widen_weight,
    narrow_weight,
    norm_gain,
    norm_bias,
    grad_out,
):
    token_low = tokens[0]
    memory_low = memory[0]
    row_in = token_low.astype(jnp.float32)
    segment_row = token_segments[0]
    places = jnp.arange(segment_row.shape[0])
    diagonal = places[None, :] == places[:, None]
    live_keys = padding[0] == 1
    self_allowed = (
        (segment_row[:, None] == segment_row[None, :])
        & (places[None, :] <= places[:, None])
        & (live_keys[None, :] | diagonal)
    )
    cross_allowed = segment_row[:, None] == memory_segments[0][None, :]
    pad_scale = padding[0].astype(jnp.float32)[:, None]
    width = token_low.shape[1]
    own = self_project.shape[1]
    hidden_width = widen_weight.shape[1]
    count, far = cube.count, cube.far
    orders = cube.orders
    side = lax.axis_index("pair")
    drive = Driver(cube, GATHER_DEPTH)

    def both_sides(mine, other):
        return [jnp.where(side == 0, mine, other), jnp.where(side == 0, other, mine)]

    shard = widen_weight.reshape(own, far, 2, hidden_width // (2 * far))
    mine, other = (
        lax.dynamic_index_in_dim(shard, k, axis=2, keepdims=False).reshape(own, hidden_width // 2)
        for k in (side, 1 - side)
    )
    narrow_shard = jnp.concatenate([narrow_weight[: 2 * own], narrow_weight[2 * own :]], axis=1)
    wide_shard = jnp.concatenate(
        [*both_sides(mine, drive.swap(other, PAIR)), narrow_shard], axis=0
    ).reshape(4, own, 2 * width)

    def gather_wide():
        return lax.all_gather(drive.after(wide_shard), ("far", "core", "fsdp"), axis=1, tiled=True)

    def gather_cross():
        return lax.all_gather(drive.after(cross_project[1:]), AXES, axis=1, tiled=True)

    norm_rows = jnp.concatenate([norm_gain, norm_bias], axis=0)
    norm_rows = jnp.pad(norm_rows, ((0, 16 - 6), (0, width - own)))
    shared = orders["A"][:2:-1]
    self_shard = jnp.concatenate([self_project.reshape(3 * own, width), self_output, norm_rows], axis=0)
    cross_shard = jnp.concatenate([cross_project[0], cross_output], axis=0)
    drive.calls = {"wide": gather_wide, "cross": gather_cross}
    drive.starts = {
        "s": lambda: cube.spread(self_shard[None], shared),
        "c": lambda: cube.spread(cross_shard[None], shared),
        "s1": lambda: cube.gather(drive.finish(["s"])[0][:, : 2 * own], orders[GATHER["s1"]]),
        "s2": lambda: cube.gather(drive.finish(["s"])[0][:, 2 * own :], orders[GATHER["s2"]]),
        "c1": lambda: cube.gather(drive.finish(["c"])[0][:, :own], orders[GATHER["c1"]]),
        "c2": lambda: cube.gather(drive.finish(["c"])[0][:, own:], orders[GATHER["c2"]]),
    }
    drive.advance(STEPS["early"])
    drive.finish(["s", "c"])
    drive.advance(STEPS["self"][:-2])
    cross_key, cross_value = lax.optimization_barrier(
        tuple(rounded(product(memory_low, weight)) for weight in drive.finish(["cross"])[0])
    )
    drive.done(cross_key)
    drive.advance(STEPS["self"][-2:])
    drive.finish(["s1", "s2"])
    query_full, key_full = cube.natural(drive.results["s1"], orders[GATHER["s1"]], [own, own], cube.place)
    value_full, self_final, norms = cube.natural(drive.results["s2"], orders[GATHER["s2"]], [own, own, 16], cube.place)
    self_stack = [query_full, key_full, value_full]
    norms = norms.reshape(count, 16, width)[:, :6, :own].transpose(1, 0, 2).reshape(6, width)
    norms = norms.astype(jnp.float32)
    gain_values, bias_values = norms[:3], norms[3:]

    self_query, self_key, self_value = project_three(token_low, token_low, self_stack)
    self_mixed, self_logsum = attend_forward(self_query, self_key, self_value, self_allowed)
    pre_one = ALPHA * row_in + product(self_mixed, self_final)
    first_out = normalize(pre_one, gain_values[0], bias_values[0])
    first_low = rounded(first_out)

    drive.done(first_low)
    drive.advance(STEPS["cross"])
    drive.finish(["c1", "c2"])
    drive.finish(["wide", "cross"])
    (query_full,) = cube.natural(drive.results["c1"], orders[GATHER["c1"]], [own], cube.place)
    (cross_final,) = cube.natural(drive.results["c2"], orders[GATHER["c2"]], [own], cube.place)
    cross_stack = [query_full, *drive.results["cross"]]
    cross_query = rounded(product(first_low, query_full))
    cross_mixed, cross_logsum = attend_forward(cross_query, cross_key, cross_value, cross_allowed)
    pre_two = ALPHA * first_out + product(cross_mixed, cross_final)
    second = normalize(pre_two, gain_values[1], bias_values[1])
    second_low = rounded(second)

    widen_full, narrow_full = cube.unpacked(drive.results["wide"])

    def widened(rows_low):
        hidden = product(rows_low, widen_full)
        active = rounded(jax.nn.gelu(hidden))
        return hidden, active, product(active, narrow_full)

    second_other = cube.swap(second_low, PAIR)
    hidden, active, branch = widened(second_low)
    hidden_other, active_other, branch_other = widened(second_other)
    branch_got = cube.swap(rounded(branch_other), PAIR)
    pre_three = ALPHA * second + (branch + branch_got.astype(jnp.float32))
    third_out = normalize(pre_three, gain_values[2], bias_values[2])
    layer_out = rounded(third_out * pad_scale)

    (self_mixed_turned,) = cube.turned([self_mixed], [orders[SCATTER["S2"]]], cube.place)
    token_turned = cube.turned([token_low], [orders[SCATTER["S1"]], orders[SCATTER["S2"]]], cube.place)
    (first_turned,) = cube.turned([first_low], [orders[SCATTER["P2"]]], cube.place)
    (memory_turned,) = cube.turned([memory_low], [orders[SCATTER["P1"]]], cube.place)
    (cross_mixed_turned,) = cube.turned([cross_mixed], [orders[SCATTER["P2"]]], cube.place)
    (second_turned,) = cube.turned([second_low, second_other], [[*orders[SCATTER["W"]], PAIR]], cube.place)
    (active_turned,) = cube.turned([active, active_other], [orders[SCATTER["N"]]], cube.side_place)
    drive = Driver(cube, SCATTER_DEPTH)

    grad_third = grad_out[0].astype(jnp.float32) * pad_scale
    grad_pre_three, grad_gain_three, grad_bias_three = normalize_back(
        pre_three, gain_values[2], bias_values[2], grad_third
    )
    ffn_branch = rounded(grad_pre_three)

    def widened_back(branch_low, hidden):
        grad_active = product(branch_low, narrow_full.T)
        unused, gelu_pull = jax.vjp(jax.nn.gelu, hidden)
        grad_hidden = rounded(gelu_pull(grad_active)[0])
        return grad_hidden, product(grad_hidden, widen_full.T)

    ffn_branch_other = cube.swap(ffn_branch, PAIR)
    grad_hidden, grad_branch = widened_back(ffn_branch, hidden)
    grad_hidden_other, grad_branch_other = widened_back(ffn_branch_other, hidden_other)
    grad_branch_got = drive.swap(drive.done(rounded(grad_branch_other)), PAIR)
    drive.add(
        "N",
        cube.scatter(
            [(drive.after(active_turned), jnp.concatenate([ffn_branch, ffn_branch_other], axis=0))], orders[SCATTER["N"]]
        ),
    )
    drive.add(
        "W",
        cube.scatter_pair(
            [(drive.after(second_turned), jnp.concatenate([grad_hidden, grad_hidden_other], axis=0))],
            orders[SCATTER["W"]],
        ),
    )
    grad_branch_got = drive.after(grad_branch_got)
    grad_second = ALPHA * grad_pre_three + (grad_branch + grad_branch_got.astype(jnp.float32))

    grad_pre_two, grad_gain_two, grad_bias_two = normalize_back(
        pre_two, gain_values[1], bias_values[1], grad_second
    )
    cross_branch = drive.done(rounded(grad_pre_two))
    drive.advance(STEPS["gs"])
    cross_branch = drive.after(cross_branch)
    grad_mixed = rounded(product(cross_branch, cross_final.T))
    cross_keys, cross_dq = attend_backward(
        cross_query, cross_key, cross_value, cross_allowed, cross_logsum, grad_mixed, (("k", "v"), ("q",))
    )
    cross_dk, cross_dv = cross_keys[:, :width], cross_keys[:, width:]
    grad_first_in, grad_memory = project_inputs(cross_stack, cross_dq, cross_dk, cross_dv)
    grad_first = ALPHA * grad_pre_two + grad_first_in
    drive.add(
        "P1",
        cube.scatter([(memory_turned, cross_keys)], orders[SCATTER["P1"]]),
    )
    drive.add(
        "P2",
        cube.scatter([(first_turned, cross_dq), (cross_mixed_turned, cross_branch)], orders[SCATTER["P2"]]),
    )
    drive.advance(STEPS["gf"])
    grad_first = drive.after(grad_first)

    grad_pre_one, grad_gain_one, grad_bias_one = normalize_back(
        pre_one, gain_values[0], bias_values[0], grad_first
    )
    self_branch = rounded(grad_pre_one)
    grad_mixed = rounded(product(self_branch, self_final.T))
    self_keys, self_dv = attend_backward(
        self_query, self_key, self_value, self_allowed, self_logsum, grad_mixed, (("q", "k"), ("v",))
    )
    self_dq, self_dk = self_keys[:, :width], self_keys[:, width:]
    grad_norms = jnp.stack(
        [
            grad_gain_one,
            grad_gain_two,
            grad_gain_three,
            grad_bias_one,
            grad_bias_two,
            grad_bias_three,
        ]
    )
    grad_norms = jnp.pad(lax.optimization_barrier(grad_norms), ((0, 128 - 6), (0, 0)))
    (norms_turned,) = cube.turned([grad_norms], [orders[SCATTER["S2"]]], cube.place)
    drive.advance(STEPS["pre"])
    drive.add(
        "S1",
        cube.scatter(
            [(drive.after(token_turned[0]), self_keys)], orders[SCATTER["S1"]]
        ),
    )
    drive.add(
        "S2",
        cube.scatter(
            [(drive.after(token_turned[1]), self_dv), (self_mixed_turned, self_branch)],
            orders[SCATTER["S2"]],
            norms_turned.reshape(width, 128),
        ),
    )
    grad_query_in, grad_key_in = project_inputs(self_stack, drive.after(self_dq), self_dk, self_dv)
    grad_tokens = ALPHA * grad_pre_one + grad_query_in + grad_key_in
    drive.advance(STEPS["tail"])
    drive.finish(["N", "W", "P1", "P2", "S1", "S2"])
    sums = drive.results
    grad_norms = sums["S2"][:, 2 * width : 2 * width + 6].T
    widen_mine, widen_other = sums["W"]
    grad_widen = jnp.stack(
        [
            block.reshape(own, far, hidden_width // (2 * far))
            for block in both_sides(widen_mine, widen_other)
        ],
        axis=2,
    ).reshape(own, hidden_width)
    return (
        layer_out[None],
        grad_tokens[None],
        grad_memory[None],
        jnp.stack([sums["S1"][:, :width], sums["S1"][:, width:], sums["S2"][:, :width]]),
        sums["S2"][:, width : 2 * width],
        jnp.stack([sums["P2"][:, :width], sums["P1"][:, :width], sums["P1"][:, width:]]),
        sums["P2"][:, width:],
        grad_widen,
        sums["N"],
        grad_norms[:3],
        grad_norms[3:],
    )


def solution(mesh):
    cube = Cube(mesh)
    return jax.shard_map(
        functools.partial(per_device, cube),
        mesh=cube.mesh,
        in_specs=(
            P(AXES, None, None),
            P(AXES, None, None),
            P(AXES, None),
            P(AXES, None),
            P(AXES, None),
            P(None, AXES, None),
            P(AXES, None),
            P(None, AXES, None),
            P(AXES, None),
            P(AXES, None),
            P(AXES, None),
            P(None, AXES),
            P(None, AXES),
            P(AXES, None, None),
        ),
        out_specs=(
            P(AXES, None, None),
            P(AXES, None, None),
            P(AXES, None, None),
            P(None, AXES, None),
            P(AXES, None),
            P(None, AXES, None),
            P(AXES, None),
            P(AXES, None),
            P(AXES, None),
            P(None, AXES),
            P(None, AXES),
        ),
        check_vma=False,
    )
```
